32 devices in a mesh: replica: 4 (over z), fsdp: 8 (over y, x, core).
Axes of the slice: x: 2, y: 2, z: 4, core: 2. Of those that a mesh axis runs over, the one named last changes fastest.
Arguments:
- grads: bfloat16 [4, 20, 704, 1024], P('replica', None, 'fsdp'), may hold values from -20 to 20
- momentum: bfloat16 [20, 704, 1024], P('replica', 'fsdp'), may hold values from -3 to 3
- weight: bfloat16 [20, 704, 1024], P('replica', 'fsdp'), may hold values from -6 to 6
- owners: int32 [20], replicated, may hold values from 0 to 8, as said below
Outputs:
- new_momentum: bfloat16 [20, 704, 1024], P('replica', 'fsdp')
- update: bfloat16 [20, 704, 1024], P('replica', 'fsdp')
- new_weight: bfloat16 [20, 704, 1024], P('replica', 'fsdp')
The draws below stay inside these ranges and needn't reach their ends.
Inputs may be any that keep to these rules, and one draw needn't show every extreme that they name: `owners`: matrices 5 * r to 5 * (r + 1) - 1 form group r. Within a group no value below 8 is named by more than 2 matrices, and some value by exactly 2.
All inputs are finite; a program needn't handle non-finite values.
Results may differ from the reference program's by a relative error of at most 0.018.
Values may be sent and summed in bfloat16 or wider, within the bound.
A program may use at most 64 MiB of HBM per device.

```python
import math
import jax
import jax.numpy as jnp
from jax import lax

D = 1024
HID = 704
ITERS = 2
CAP = 2
MPG = 5
MATS = 20
N_REPLICA = 4
N_FSDP = 8


def draw_grads(key, part):
    key = jax.random.fold_in(key, 5)
    key_rows, key_cols, key_own = jax.random.split(key, 3)
    shape = (N_REPLICA, MATS, HID, D)
    row_scale = jnp.exp(jax.random.uniform(key_rows, (1, MATS, HID, 1), jnp.float32, math.log(0.3), math.log(3.0)))
    col_scale = jnp.exp(jax.random.uniform(key_cols, (1, MATS, 1, D), jnp.float32, math.log(0.3), math.log(3.0)))
    noise = jnp.clip(jax.random.normal(key_own, shape, jnp.float32), -6.0, 6.0)
    return (0.35 * noise * row_scale * col_scale).astype(jnp.bfloat16)


def draw_owners(key, part):
    key = jax.random.fold_in(key, 11)
    group_keys = jax.random.split(key, N_REPLICA)

    def one_group(group_key):
        perm_key, frozen_key, order_key = jax.random.split(group_key, 3)
        shuffled = jax.random.permutation(perm_key, N_FSDP * CAP)
        slot_ids = shuffled[:MPG]
        first = slot_ids[0]
        partner = first // CAP * CAP + (first % CAP + 1) % CAP
        position = jnp.arange(MPG)
        slot_ids = jnp.where((slot_ids == partner) & (position > 0), slot_ids[1], slot_ids)
        slot_ids = jnp.where(position == 1, partner, slot_ids)
        owner_ids = slot_ids // CAP
        frozen = (jax.random.randint(frozen_key, (MPG,), 0, 10) == 0) & (position >= 2)
        owner_ids = jnp.where(frozen, N_FSDP, owner_ids)
        order = jax.random.permutation(order_key, MPG)
        return owner_ids[order].astype(jnp.int32)
    return jax.vmap(one_group)(group_keys).reshape(MATS).astype(jnp.int32)


def block_levels(own_key, dims, cuts, low, high):
    gain, own = 1.0, jax.random.fold_in(own_key, 6)
    for dim, parts in cuts:
        draws = jnp.exp(jax.random.uniform(jax.random.fold_in(own, dim), (parts,), jnp.float32, low / len(cuts), high / len(cuts)))
        gain = gain * jnp.repeat(draws, dims[dim] // parts).reshape([-1 if axis == dim else 1 for axis in range(len(dims))])
    return gain


def bell_draw(own_key, shape, width, bound, cuts=(), held_as=jnp.bfloat16):
    result = jax.random.normal(own_key, shape, jnp.float32) * width
    if len(cuts) > 0:
        result = block_levels(own_key, shape, cuts, -0.22, 0.18) * result
    return jnp.clip(result, min=-bound, max=bound).astype(held_as)


def setup_inputs(seed: int = 0) -> dict:
    key_list = jax.random.split(jax.random.key(seed), 5)
    grads = draw_grads(jax.random.fold_in(key_list[4], 71), 0)
    momentum = bell_draw(key_list[1], (MATS, HID, D), 0.5, 3.0, ((0, 4), (1, 8)))
    weight = bell_draw(key_list[2], (MATS, HID, D), 1.0, 6.0, ((0, 4), (1, 8)))
    owners = draw_owners(jax.random.fold_in(key_list[4], 71), 0)
    return dict(grads=grads, momentum=momentum, weight=weight, owners=owners)


EPSILON = 1e-07
COEFF_LINEAR = 3.4445
COEFF_CUBIC = -4.775
COEFF_QUINTIC = 2.0315
MOMENTUM_DECAY = 0.95
LEARN_RATE = 0.02
DECAY_RATE = 0.1
UPDATE_RATIO = 0.2

def newton_schulz(matrix):
    scaled = matrix.astype(jnp.float32)
    frobenius = jnp.sqrt(jnp.sum(scaled * scaled))
    iterate = lax.optimization_barrier((scaled / (frobenius + EPSILON)).astype(jnp.bfloat16))
    for turn in range(ITERS):
        gram_matrix = jnp.dot(iterate, iterate.T, preferred_element_type=jnp.float32).astype(jnp.bfloat16)
        gram_matrix = lax.optimization_barrier(gram_matrix)
        gram_square = jnp.dot(gram_matrix, gram_matrix, preferred_element_type=jnp.float32)
        poly_term = (COEFF_CUBIC * gram_matrix.astype(jnp.float32) + COEFF_QUINTIC * gram_square).astype(jnp.bfloat16)
        iterate = (COEFF_LINEAR * iterate.astype(jnp.float32) + jnp.dot(poly_term, iterate, preferred_element_type=jnp.float32)).astype(jnp.bfloat16)
        iterate = lax.optimization_barrier(iterate)
    return iterate

def reference(grads, momentum, weight, owners):
    summed = lax.optimization_barrier(jnp.sum(grads.astype(jnp.float32), axis=0))
    active = (owners < N_FSDP)[:, None, None]
    old_momentum = momentum.astype(jnp.float32)
    new_momentum = jnp.where(active, MOMENTUM_DECAY * old_momentum + summed, old_momentum).astype(jnp.bfloat16)
    stored = lax.optimization_barrier(new_momentum)
    nesterov = (summed + MOMENTUM_DECAY * stored.astype(jnp.float32)).astype(jnp.bfloat16)
    orthogonal = lax.map(newton_schulz, nesterov)
    orthogonal = jnp.where(active, orthogonal.astype(jnp.float32), jnp.float32(0.0))
    update_scale = UPDATE_RATIO * math.sqrt(max(HID, D))
    update = (update_scale * orthogonal).astype(jnp.bfloat16)
    old_weight = weight.astype(jnp.float32)
    stepped = old_weight * (1.0 - LEARN_RATE * DECAY_RATE) - LEARN_RATE * update_scale * orthogonal
    new_weight = jnp.where(active, stepped, old_weight).astype(jnp.bfloat16)
    return (new_momentum, update, new_weight)
```

```python
import functools
import math

import jax
import jax.numpy as jnp
from jax import lax
from jax.experimental import pallas as pl
from jax.experimental.pallas import tpu as pltpu
from jax.sharding import PartitionSpec as P

ITERS = 2
ROW_TILE = 8
KERNEL_VMEM = 56 * 1024 * 1024


EPSILON = 1e-07
COEFF_LINEAR = 3.4445
COEFF_CUBIC = -4.775
COEFF_QUINTIC = 2.0315
MOMENTUM_DECAY = 0.95
LEARN_RATE = 0.02
DECAY_RATE = 0.1
UPDATE_RATIO = 0.2


def newton_blocks(blocks):
    scaled = blocks.astype(jnp.float32)
    frobenius = jnp.sqrt(jnp.sum(scaled * scaled, axis=(1, 2), keepdims=True))
    iterate = lax.optimization_barrier((scaled / (frobenius + EPSILON)).astype(jnp.bfloat16))
    for turn in range(ITERS):
        gram_matrix = jnp.einsum(
            "cik,cjk->cij", iterate, iterate, preferred_element_type=jnp.float32
        ).astype(jnp.bfloat16)
        gram_matrix = lax.optimization_barrier(gram_matrix)
        gram_square = jnp.einsum(
            "cij,cjk->cik", gram_matrix, gram_matrix, preferred_element_type=jnp.float32
        )
        poly_term = (
            COEFF_CUBIC * gram_matrix.astype(jnp.float32) + COEFF_QUINTIC * gram_square
        ).astype(jnp.bfloat16)
        product = jnp.einsum("cij,cjk->cik", poly_term, iterate, preferred_element_type=jnp.float32)
        iterate = (COEFF_LINEAR * iterate.astype(jnp.float32) + product).astype(jnp.bfloat16)
        iterate = lax.optimization_barrier(iterate)
    return iterate


def add_rows(left, right):
    return left.astype(jnp.float32) + right.astype(jnp.float32)


def fused_kernel(
    n_rep,
    n_fsdp,
    count,
    coef_ref,
    grads_ref,
    momentum_ref,
    stored_out,
    orth_out,
    own,
    old,
    from_left,
    from_right,
    total,
    stored,
    outgoing,
    gathered,
    iterate,
    gram,
    poly,
    finished,
    returned,
    load_sem,
    right_send,
    right_recv,
    left_send,
    left_recv,
    gather_send,
    gather_recv,
    return_send,
    return_recv,
    out_sem,
):
    rep = lax.axis_index("replica")
    me = lax.axis_index("fsdp")
    row_count, col_count = own.shape[1:]
    chips = n_fsdp // 2

    def owner_of(mat):
        return lax.rem(mat, chips) * 2 + mat // chips

    mine = lax.rem(me, 2) * chips + me // 2
    is_owner = mine < count
    turn_of_mine = jnp.where(
        mine < count - 3, mine + 1, jnp.where(mine < count - 1, count - 1, count)
    )

    load_grads = pltpu.make_async_copy(grads_ref, own, load_sem.at[0])
    load_old = pltpu.make_async_copy(momentum_ref, old, load_sem.at[1])
    load_grads.start()
    load_old.start()

    barrier = pltpu.get_barrier_semaphore()
    for step in range(1, n_fsdp):
        pl.semaphore_signal(barrier, inc=1, device_id={"fsdp": lax.rem(me + step, n_fsdp)})

    @pl.when(rep > 0)
    def _():
        pl.semaphore_signal(barrier, inc=1, device_id={"replica": rep - 1})

    @pl.when(rep < n_rep - 1)
    def _():
        pl.semaphore_signal(barrier, inc=1, device_id={"replica": rep + 1})

    inner = (rep > 0) & (rep < n_rep - 1)
    pl.semaphore_wait(barrier, jnp.where(inner, n_fsdp + 1, n_fsdp))

    load_grads.wait()
    load_old.wait()

    def right_copy(group, mat, raw=False):
        return pltpu.make_async_remote_copy(
            src_ref=own.at[group * count + mat] if raw else from_left.at[group, mat],
            dst_ref=from_left.at[group, mat],
            send_sem=right_send.at[group, mat],
            recv_sem=right_recv.at[group, mat],
            device_id={"replica": rep + 1},
        )

    def left_copy(group, mat, raw=False):
        return pltpu.make_async_remote_copy(
            src_ref=own.at[group * count + mat] if raw else from_right.at[group, mat],
            dst_ref=from_right.at[group, mat],
            send_sem=left_send.at[group, mat],
            recv_sem=left_recv.at[group, mat],
            device_id={"replica": rep - 1},
        )

    def gather_copy(mat, slot):
        return pltpu.make_async_remote_copy(
            src_ref=outgoing.at[mat],
            dst_ref=gathered.at[slot],
            send_sem=gather_send.at[mat],
            recv_sem=gather_recv.at[slot],
            device_id={"fsdp": owner_of(mat)},
        )

    def return_copy(mat, slot):
        return pltpu.make_async_remote_copy(
            src_ref=finished.at[slot],
            dst_ref=returned.at[mat],
            send_sem=return_send.at[slot],
            recv_sem=return_recv.at[mat],
            device_id={"fsdp": slot},
        )

    def stored_copy(mat):
        return pltpu.make_async_copy(stored.at[mat], stored_out.at[mat], out_sem.at[0, mat])

    def orth_copy(mat):
        return pltpu.make_async_copy(returned.at[mat], orth_out.at[mat], out_sem.at[1, mat])

    def send_raw(mat):
        @pl.when(rep == 0)
        def _():
            for group in range(n_rep - 1, 0, -1):
                right_copy(group, mat, raw=True).start()

        @pl.when(rep == n_rep - 1)
        def _():
            for group in range(n_rep - 1):
                left_copy(group, mat, raw=True).start()

    def forward(mat):
        for step in range(n_rep - 1):
            high, low = n_rep - 1 - step, step

            @pl.when((rep > 0) & (rep < high))
            def _():
                right_copy(high, mat).wait_recv()
                from_left[high, mat] = add_rows(
                    from_left[high, mat], own[high * count + mat]
                ).astype(jnp.bfloat16)
                right_copy(high, mat).start()

            @pl.when((rep < n_rep - 1) & (rep > low))
            def _():
                left_copy(low, mat).wait_recv()
                from_right[low, mat] = add_rows(
                    from_right[low, mat], own[low * count + mat]
                ).astype(jnp.bfloat16)
                left_copy(low, mat).start()

    def finish_sum(mat):
        total[...] = own[rep * count + mat].astype(jnp.float32)

        @pl.when(rep > 0)
        def _():
            right_copy(rep, mat).wait_recv()
            total[...] += from_left[rep, mat].astype(jnp.float32)

        @pl.when(rep < n_rep - 1)
        def _():
            left_copy(rep, mat).wait_recv()
            total[...] += from_right[rep, mat].astype(jnp.float32)

        summed = total[...]
        kept = (coef_ref[0, mat] * old[mat].astype(jnp.float32) + coef_ref[1, mat] * summed).astype(
            jnp.bfloat16
        )
        stored[mat] = kept
        stored_copy(mat).start()
        outgoing[mat] = (summed + MOMENTUM_DECAY * kept.astype(jnp.float32)).astype(jnp.bfloat16)

        @pl.when(me == owner_of(mat))
        def _():
            gathered[me] = outgoing[mat]

        @pl.when(me != owner_of(mat))
        def _():
            gather_copy(mat, me).start()

    def orthogonalize():
        @pl.loop(1, n_fsdp)
        def _(step):
            gather_copy(mine, lax.rem(me + step, n_fsdp)).wait_recv()

        scaled = gathered[...].astype(jnp.float32)
        frobenius = jnp.sqrt(jnp.sum(scaled * scaled))
        inverse = 1.0 / (frobenius + EPSILON)
        iterate[...] = (
            (scaled * inverse).reshape(n_fsdp * row_count, col_count).astype(jnp.bfloat16)
        )

        def newton(last):
            held = iterate[...]
            gram[...] = lax.dot_general(
                held, held, (((1,), (1,)), ((), ())), preferred_element_type=jnp.float32
            ).astype(jnp.bfloat16)
            square = jnp.dot(gram[...], gram[...], preferred_element_type=jnp.float32)
            poly[...] = (
                COEFF_CUBIC * gram[...].astype(jnp.float32) + COEFF_QUINTIC * square
            ).astype(jnp.bfloat16)
            product = jnp.dot(poly[...], iterate[...], preferred_element_type=jnp.float32)
            result = COEFF_LINEAR * iterate[...].astype(jnp.float32) + product
            if last:
                finished[...] = result.reshape(n_fsdp, row_count, col_count).astype(jnp.bfloat16)
            else:
                iterate[...] = result.astype(jnp.bfloat16)

        for turn in range(ITERS):
            newton(turn == ITERS - 1)

        @pl.loop(1, n_fsdp)
        def _(step):
            return_copy(mine, lax.rem(me + step, n_fsdp)).start()

        returned[mine] = finished[me]

    send_raw(0)

    @pl.loop(0, count + 1)
    def _(turn):
        @pl.when(turn < count - 1)
        def _():
            send_raw(turn + 1)

        @pl.when(turn < count)
        def _():
            forward(turn)
            finish_sum(turn)

        @pl.when(is_owner & (turn == turn_of_mine))
        def _():
            orthogonalize()

    @pl.loop(0, count)
    def _(mat):
        @pl.when(me != owner_of(mat))
        def _():
            return_copy(mat, me).wait_recv()

        orth_copy(mat).start()

    @pl.loop(0, count)
    def _(mat):
        for group in range(n_rep):

            @pl.when(rep < group)
            def _():
                right_copy(group, mat).wait_send()

            @pl.when(rep > group)
            def _():
                left_copy(group, mat).wait_send()

        @pl.when(me != owner_of(mat))
        def _():
            gather_copy(mat, me).wait_send()

        stored_copy(mat).wait()
        orth_copy(mat).wait()

    @pl.when(is_owner)
    def _():
        @pl.loop(1, n_fsdp)
        def _(step):
            return_copy(mine, lax.rem(me + step, n_fsdp)).wait_send()


def fused_sum_and_orthogonalize(n_rep, n_fsdp, coefs, grads, momentum):
    count, row_count, col_count = momentum.shape
    all_rows = n_fsdp * row_count
    block = (row_count, col_count)
    half = jnp.bfloat16
    shape = jax.ShapeDtypeStruct(momentum.shape, half)
    dma = pltpu.SemaphoreType.DMA
    return pl.pallas_call(
        functools.partial(fused_kernel, n_rep, n_fsdp, count),
        out_shape=(shape, shape),
        in_specs=[
            pl.BlockSpec(memory_space=pltpu.SMEM),
            pl.BlockSpec(memory_space=pl.ANY),
            pl.BlockSpec(memory_space=pl.ANY),
        ],
        out_specs=(pl.BlockSpec(memory_space=pl.ANY), pl.BlockSpec(memory_space=pl.ANY)),
        scratch_shapes=[
            pltpu.VMEM((n_rep * count, *block), half),
            pltpu.VMEM((count, *block), half),
            pltpu.VMEM((n_rep, count, *block), half),
            pltpu.VMEM((n_rep, count, *block), half),
            pltpu.VMEM(block, jnp.float32),
            pltpu.VMEM((count, *block), half),
            pltpu.VMEM((count, *block), half),
            pltpu.VMEM((n_fsdp, *block), half),
            pltpu.VMEM((all_rows, col_count), half),
            pltpu.VMEM((all_rows, all_rows), half),
            pltpu.VMEM((all_rows, all_rows), half),
            pltpu.VMEM((n_fsdp, *block), half),
            pltpu.VMEM((count, *block), half),
            dma((2,)),
            dma((n_rep, count)),
            dma((n_rep, count)),
            dma((n_rep, count)),
            dma((n_rep, count)),
            dma((count,)),
            dma((n_fsdp,)),
            dma((n_fsdp,)),
            dma((count,)),
            dma((2, count)),
        ],
        compiler_params=pltpu.CompilerParams(
            collective_id=0, has_side_effects=True, vmem_limit_bytes=KERNEL_VMEM
        ),
        name="sum_and_orthogonalize",
    )(coefs, grads, momentum)


def finish_kernel(coef_ref, stored_ref, orth_ref, weight_ref, momentum_out, update_out, weight_out):
    mat = pl.program_id(0)
    momentum_out[...] = stored_ref[...]
    orth = orth_ref[...].astype(jnp.float32)
    update_out[...] = (coef_ref[2, mat] * orth).astype(jnp.bfloat16)
    weight_out[...] = (
        coef_ref[3, mat] * weight_ref[...].astype(jnp.float32) - coef_ref[4, mat] * orth
    ).astype(jnp.bfloat16)


def finish(coefs, stored, orth, weight):
    count, row_count, col_count = weight.shape
    block = pl.BlockSpec((1, row_count, col_count), lambda mat: (mat, 0, 0))
    shape = jax.ShapeDtypeStruct(weight.shape, jnp.bfloat16)
    return pl.pallas_call(
        finish_kernel,
        grid=(count,),
        out_shape=(shape, shape, shape),
        in_specs=[pl.BlockSpec(memory_space=pltpu.SMEM), block, block, block],
        out_specs=(block, block, block),
        name="finish",
    )(coefs, stored, orth, weight)


def coefficients(active, update_scale):
    on = active.astype(jnp.float32)
    return jnp.stack(
        [
            jnp.where(active, MOMENTUM_DECAY, 1.0),
            on,
            update_scale * on,
            jnp.where(active, 1.0 - LEARN_RATE * DECAY_RATE, 1.0),
            LEARN_RATE * update_scale * on,
        ]
    )


def by_collectives(grads, momentum, weight, active, update_scale):
    groups = lax.axis_size("fsdp")
    summed = lax.psum_scatter(
        grads[0], "replica", scatter_dimension=0, tiled=True
    ).astype(jnp.float32)
    local_count, row_count, col_count = momentum.shape
    keep_mask = active[:, None, None]
    old_momentum = momentum.astype(jnp.float32)
    new_momentum = jnp.where(
        keep_mask, MOMENTUM_DECAY * old_momentum + summed, old_momentum
    ).astype(jnp.bfloat16)
    stored = lax.optimization_barrier(new_momentum)
    outgoing = (summed + MOMENTUM_DECAY * stored.astype(jnp.float32)).astype(jnp.bfloat16)
    slots = -(-local_count // groups)
    padding = slots * groups - local_count
    packed = jnp.pad(outgoing, ((0, padding), (0, 0), (0, 0)))
    received = lax.all_to_all(packed, "fsdp", split_axis=0, concat_axis=1, tiled=True)
    orthogonal = newton_blocks(received)
    returned = lax.all_to_all(orthogonal, "fsdp", split_axis=1, concat_axis=0, tiled=True)
    restored = jnp.where(keep_mask, returned[:local_count].astype(jnp.float32), 0.0)
    update = (update_scale * restored).astype(jnp.bfloat16)
    old_weight = weight.astype(jnp.float32)
    stepped = old_weight * (1.0 - LEARN_RATE * DECAY_RATE) - LEARN_RATE * update_scale * restored
    new_weight = jnp.where(keep_mask, stepped, old_weight).astype(jnp.bfloat16)
    return (new_momentum, update, new_weight)


def on_device(grads, momentum, weight, owners):
    n_fsdp = lax.axis_size("fsdp")
    n_rep = lax.axis_size("replica")
    count, row_count, col_count = momentum.shape
    update_scale = UPDATE_RATIO * math.sqrt(max(row_count * n_fsdp, col_count))
    offset = lax.axis_index("replica") * count
    active = lax.dynamic_slice_in_dim(owners, offset, count) < n_fsdp
    held_bytes = 2 * row_count * col_count * (3 * n_rep * count + 4 * count + 4 * n_fsdp)
    fits = held_bytes * 2 < KERNEL_VMEM * 3 // 2 and row_count % ROW_TILE == 0
    if not fits or n_fsdp % 2 or count > n_fsdp or n_rep < 2 or count < 3:
        return by_collectives(grads, momentum, weight, active, update_scale)
    coefs = coefficients(active, update_scale)
    stored, orth = fused_sum_and_orthogonalize(n_rep, n_fsdp, coefs, grads[0], momentum)
    return finish(coefs, stored, orth, weight)


def solution(mesh):
    in_specs = (
        P("replica", None, "fsdp", None),
        P("replica", "fsdp", None),
        P("replica", "fsdp", None),
        P(),
    )
    out_specs = (P("replica", "fsdp", None), P("replica", "fsdp", None), P("replica", "fsdp", None))
    return jax.shard_map(
        on_device, mesh=mesh, in_specs=in_specs, out_specs=out_specs, check_vma=False
    )
```

```python
import functools
import math

import jax
import jax.numpy as jnp
from jax import lax
from jax.experimental import pallas as pl
from jax.experimental.pallas import tpu as pltpu
from jax.sharding import PartitionSpec as P

ITERS = 2
ROW_TILE = 8
KERNEL_VMEM = 56 * 1024 * 1024
PARTS = 4
LOOK_AHEAD = 4
GATHER_TURNS = 3


EPSILON = 1e-07
COEFF_LINEAR = 3.4445
COEFF_CUBIC = -4.775
COEFF_QUINTIC = 2.0315
MOMENTUM_DECAY = 0.95
LEARN_RATE = 0.02
DECAY_RATE = 0.1
UPDATE_RATIO = 0.2


def newton_blocks(blocks):
    scaled = blocks.astype(jnp.float32)
    frobenius = jnp.sqrt(jnp.sum(scaled * scaled, axis=(1, 2), keepdims=True))
    iterate = lax.optimization_barrier((scaled / (frobenius + EPSILON)).astype(jnp.bfloat16))
    for turn in range(ITERS):
        gram_matrix = jnp.einsum(
            "cik,cjk->cij", iterate, iterate, preferred_element_type=jnp.float32
        ).astype(jnp.bfloat16)
        gram_matrix = lax.optimization_barrier(gram_matrix)
        gram_square = jnp.einsum(
            "cij,cjk->cik", gram_matrix, gram_matrix, preferred_element_type=jnp.float32
        )
        poly_term = (
            COEFF_CUBIC * gram_matrix.astype(jnp.float32) + COEFF_QUINTIC * gram_square
        ).astype(jnp.bfloat16)
        product = jnp.einsum("cij,cjk->cik", poly_term, iterate, preferred_element_type=jnp.float32)
        iterate = (COEFF_LINEAR * iterate.astype(jnp.float32) + product).astype(jnp.bfloat16)
        iterate = lax.optimization_barrier(iterate)
    return iterate


def add_rows(left, right):
    return left.astype(jnp.float32) + right.astype(jnp.float32)


def fused_kernel(
    n_rep,
    n_fsdp,
    count,
    owners_ref,
    grads_ref,
    momentum_ref,
    stored_out,
    orth_out,
    own,
    old,
    from_left,
    from_right,
    total,
    stored,
    outgoing,
    gathered,
    iterate,
    gram,
    poly,
    finished,
    returned,
    load_sem,
    right_send,
    right_recv,
    left_send,
    left_recv,
    gather_send,
    gather_recv,
    return_send,
    return_recv,
    out_sem,
):
    rep = lax.axis_index("replica")
    me = lax.axis_index("fsdp")
    row_count, col_count = own.shape[1:]
    width = col_count // PARTS
    units = count * PARTS
    chips = n_fsdp // 2
    early_count = count - 2
    chip, core = me // 2, lax.rem(me, 2)
    partner = me + 1 - 2 * core

    has_early = (core == 1) & (chip < early_count)

    def early_owner(mat):
        return mat * 2 + 1

    def columns(part):
        return pl.ds(pl.multiple_of(part * width, 128), width)

    load_grads = pltpu.make_async_copy(grads_ref, own, load_sem.at[0])
    load_old = pltpu.make_async_copy(momentum_ref, old, load_sem.at[1])
    load_grads.start()
    load_old.start()

    barrier = pltpu.get_barrier_semaphore()
    for step in range(1, n_fsdp):
        pl.semaphore_signal(barrier, inc=1, device_id={"fsdp": lax.rem(me + step, n_fsdp)})

    @pl.when(rep > 0)
    def _():
        pl.semaphore_signal(barrier, inc=1, device_id={"replica": rep - 1})

    @pl.when(rep < n_rep - 1)
    def _():
        pl.semaphore_signal(barrier, inc=1, device_id={"replica": rep + 1})

    inner = (rep > 0) & (rep < n_rep - 1)
    pl.semaphore_wait(barrier, jnp.where(inner, n_fsdp + 1, n_fsdp))
    load_grads.wait()
    load_old.wait()

    def right_copy(group, unit, raw=False):
        mat, cols = unit // PARTS, columns(lax.rem(unit, PARTS))
        held = own.at[group * count + mat] if raw else from_left.at[group, mat]
        return pltpu.make_async_remote_copy(
            src_ref=held.at[:, cols],
            dst_ref=from_left.at[group, mat, :, cols],
            send_sem=right_send.at[group, unit],
            recv_sem=right_recv.at[group, unit],
            device_id={"replica": rep + 1},
        )

    def left_copy(group, unit, raw=False):
        mat, cols = unit // PARTS, columns(lax.rem(unit, PARTS))
        held = own.at[group * count + mat] if raw else from_right.at[group, mat]
        return pltpu.make_async_remote_copy(
            src_ref=held.at[:, cols],
            dst_ref=from_right.at[group, mat, :, cols],
            send_sem=left_send.at[group, unit],
            recv_sem=left_recv.at[group, unit],
            device_id={"replica": rep - 1},
        )

    def gather_copy(unit, job, slot, target, place):
        mat, part = unit // PARTS, lax.rem(unit, PARTS)
        cols = columns(part)
        return pltpu.make_async_remote_copy(
            src_ref=outgoing.at[mat, :, cols],
            dst_ref=gathered.at[job, slot, :, cols],
            send_sem=gather_send.at[unit, place],
            recv_sem=gather_recv.at[job, slot, part],
            device_id={"fsdp": target},
        )

    def return_copy(job, mat, slot):
        return pltpu.make_async_remote_copy(
            src_ref=finished.at[job, slot],
            dst_ref=returned.at[mat],
            send_sem=return_send.at[job, slot],
            recv_sem=return_recv.at[mat],
            device_id={"fsdp": slot},
        )

    def stored_copy(mat):
        return pltpu.make_async_copy(stored.at[mat], stored_out.at[mat], out_sem.at[0, mat])

    def orth_copy(mat):
        return pltpu.make_async_copy(returned.at[mat], orth_out.at[mat], out_sem.at[1, mat])

    def send_raw(unit):
        @pl.when(rep == 0)
        def _():
            for group in range(n_rep - 1, 0, -1):
                right_copy(group, unit, raw=True).start()

        @pl.when(rep == n_rep - 1)
        def _():
            for group in range(n_rep - 1):
                left_copy(group, unit, raw=True).start()

    def forward(unit):
        mat, cols = unit // PARTS, columns(lax.rem(unit, PARTS))
        for step in range(n_rep - 1):
            high, low = n_rep - 1 - step, step

            @pl.when((rep > 0) & (rep < high))
            def _():
                right_copy(high, unit).wait_recv()
                from_left[high, mat, :, cols] = add_rows(
                    from_left[high, mat, :, cols], own[high * count + mat, :, cols]
                ).astype(jnp.bfloat16)
                right_copy(high, unit).start()

            @pl.when((rep < n_rep - 1) & (rep > low))
            def _():
                left_copy(low, unit).wait_recv()
                from_right[low, mat, :, cols] = add_rows(
                    from_right[low, mat, :, cols], own[low * count + mat, :, cols]
                ).astype(jnp.bfloat16)
                left_copy(low, unit).start()

    def each_gather(unit, act):
        mat = unit // PARTS
        late_core = mat - early_count

        @pl.when((mat < early_count) & (me != early_owner(mat)))
        def _():
            act(gather_copy(unit, 0, me, early_owner(mat), 0))

        @pl.when(mat >= early_count)
        def _():
            for step in range(1, chips):
                target = lax.rem(chip + step, chips) * 2 + late_core
                act(gather_copy(unit, 1, me, target, step))

            @pl.when(core != late_core)
            def _():
                act(gather_copy(unit, 1, me, partner, 0))

    def finish_sum(unit):
        mat, cols = unit // PARTS, columns(lax.rem(unit, PARTS))
        total[...] = own[rep * count + mat, :, cols].astype(jnp.float32)

        @pl.when(rep > 0)
        def _():
            right_copy(rep, unit).wait_recv()
            total[...] += from_left[rep, mat, :, cols].astype(jnp.float32)

        @pl.when(rep < n_rep - 1)
        def _():
            left_copy(rep, unit).wait_recv()
            total[...] += from_right[rep, mat, :, cols].astype(jnp.float32)

        summed = total[...]
        active = owners_ref[rep * count + mat] < n_fsdp
        decay = jnp.where(active, jnp.float32(MOMENTUM_DECAY), jnp.float32(1.0))
        gain = jnp.where(active, jnp.float32(1.0), jnp.float32(0.0))
        kept = (decay * old[mat, :, cols].astype(jnp.float32) + gain * summed).astype(jnp.bfloat16)
        stored[mat, :, cols] = kept
        nesterov = (summed + MOMENTUM_DECAY * kept.astype(jnp.float32)).astype(jnp.bfloat16)
        outgoing[mat, :, cols] = nesterov

        @pl.when((mat < early_count) & (me == early_owner(mat)))
        def _():
            gathered[0, me, :, cols] = nesterov

        @pl.when((mat >= early_count) & (core == mat - early_count))
        def _():
            gathered[1, me, :, cols] = nesterov

        each_gather(unit, lambda copy: copy.start())

        @pl.when(lax.rem(unit, PARTS) == PARTS - 1)
        def _():
            stored_copy(mat).start()

    def make_gram():
        held = iterate[...]
        gram[...] = lax.dot_general(
            held, held, (((1,), (1,)), ((), ())), preferred_element_type=jnp.float32
        ).astype(jnp.bfloat16)

    def make_poly(rows):
        square = jnp.dot(gram[rows, :], gram[...], preferred_element_type=jnp.float32)
        poly[rows, :] = (
            COEFF_CUBIC * gram[rows, :].astype(jnp.float32) + COEFF_QUINTIC * square
        ).astype(jnp.bfloat16)

    def apply_poly(rows):
        product = jnp.dot(poly[rows, :], iterate[...], preferred_element_type=jnp.float32)
        return COEFF_LINEAR * iterate[rows, :].astype(jnp.float32) + product

    def orthogonalize(job, mat):
        @pl.loop(1, n_fsdp)
        def _(step):
            for part in range(PARTS):
                unit = mat * PARTS + part
                gather_copy(unit, job, lax.rem(me + step, n_fsdp), me, 0).wait_recv()

        scaled = gathered[job].astype(jnp.float32)
        frobenius = jnp.sqrt(jnp.sum(scaled * scaled))
        inverse = 1.0 / (frobenius + EPSILON)
        iterate[...] = (
            (scaled * inverse).reshape(n_fsdp * row_count, col_count).astype(jnp.bfloat16)
        )
        whole = pl.ds(0, n_fsdp * row_count)
        for turn in range(ITERS - 1):
            make_gram()
            make_poly(whole)
            iterate[...] = apply_poly(whole).astype(jnp.bfloat16)
        make_gram()

        @pl.when(job == 0)
        def _():
            make_poly(whole)
            finished[0] = (
                apply_poly(whole).reshape(n_fsdp, row_count, col_count).astype(jnp.bfloat16)
            )

            @pl.loop(1, n_fsdp)
            def _(step):
                return_copy(0, mat, lax.rem(me + step, n_fsdp)).start()

            returned[mat] = finished[0, me]

        @pl.when(job == 1)
        def _():
            pair = pl.ds(pl.multiple_of(chip * (2 * row_count), 16), 2 * row_count)
            make_poly(pair)
            rows = apply_poly(pair).reshape(2, row_count, col_count).astype(jnp.bfloat16)
            finished[1, pl.ds(chip * 2, 2)] = rows
            return_copy(1, mat, partner).start()
            returned[mat] = finished[1, me]

    ahead = LOOK_AHEAD
    for unit in range(ahead):
        send_raw(unit)

    @pl.loop(0, units)
    def _(turn):
        @pl.when(turn < units - ahead)
        def _():
            send_raw(turn + ahead)

        forward(turn)
        finish_sum(turn)
        last = turn == units - 1
        early = has_early & (turn == (chip + 1) * PARTS - 1 + GATHER_TURNS)

        @pl.when(last | early)
        def _():
            job = jnp.where(last, 1, 0)
            orthogonalize(job, jnp.where(last, early_count + core, chip))

    @pl.loop(0, count)
    def _(mat):
        held_here = jnp.where(
            mat < early_count, me == early_owner(mat), core == mat - early_count
        )

        @pl.when(jnp.logical_not(held_here))
        def _():
            return_copy(0, mat, me).wait_recv()

        orth_copy(mat).start()

    @pl.loop(0, units)
    def _(unit):
        for group in range(n_rep):

            @pl.when(rep < group)
            def _():
                right_copy(group, unit).wait_send()

            @pl.when(rep > group)
            def _():
                left_copy(group, unit).wait_send()

        each_gather(unit, lambda copy: copy.wait_send())

    @pl.loop(0, count)
    def _(mat):
        stored_copy(mat).wait()
        orth_copy(mat).wait()

    @pl.when(has_early)
    def _():
        @pl.loop(1, n_fsdp)
        def _(step):
            return_copy(0, chip, lax.rem(me + step, n_fsdp)).wait_send()

    return_copy(1, early_count + core, partner).wait_send()


def fused_sum_and_orthogonalize(n_rep, n_fsdp, owners, grads, momentum):
    count, row_count, col_count = momentum.shape
    all_rows = n_fsdp * row_count
    units = count * PARTS
    block = (row_count, col_count)
    half = jnp.bfloat16
    shape = jax.ShapeDtypeStruct(momentum.shape, half)
    dma = pltpu.SemaphoreType.DMA
    return pl.pallas_call(
        functools.partial(fused_kernel, n_rep, n_fsdp, count),
        out_shape=(shape, shape),
        in_specs=[
            pl.BlockSpec(memory_space=pltpu.SMEM),
            pl.BlockSpec(memory_space=pl.ANY),
            pl.BlockSpec(memory_space=pl.ANY),
        ],
        out_specs=(pl.BlockSpec(memory_space=pl.ANY), pl.BlockSpec(memory_space=pl.ANY)),
        scratch_shapes=[
            pltpu.VMEM((n_rep * count, *block), half),
            pltpu.VMEM((count, *block), half),
            pltpu.VMEM((n_rep, count, *block), half),
            pltpu.VMEM((n_rep, count, *block), half),
            pltpu.VMEM((row_count, col_count // PARTS), jnp.float32),
            pltpu.VMEM((count, *block), half),
            pltpu.VMEM((count, *block), half),
            pltpu.VMEM((2, n_fsdp, *block), half),
            pltpu.VMEM((all_rows, col_count), half),
            pltpu.VMEM((all_rows, all_rows), half),
            pltpu.VMEM((all_rows, all_rows), half),
            pltpu.VMEM((2, n_fsdp, *block), half),
            pltpu.VMEM((count, *block), half),
            dma((2,)),
            dma((n_rep, units)),
            dma((n_rep, units)),
            dma((n_rep, units)),
            dma((n_rep, units)),
            dma((units, n_fsdp // 2)),
            dma((2, n_fsdp, PARTS)),
            dma((2, n_fsdp)),
            dma((count,)),
            dma((2, count)),
        ],
        compiler_params=pltpu.CompilerParams(
            collective_id=0, has_side_effects=True, vmem_limit_bytes=KERNEL_VMEM
        ),
        name="sum_and_orthogonalize",
    )(owners, grads, momentum)


def finish_kernel(
    n_fsdp,
    update_scale,
    owners_ref,
    stored_ref,
    orth_ref,
    weight_ref,
    momentum_out,
    update_out,
    weight_out,
    stored,
    orth,
    weight,
    update,
    stepped,
    in_sem,
    out_sem,
):
    count = weight_ref.shape[0]
    offset = lax.axis_index("replica") * count
    loads, stores = [], []
    for mat in range(count):
        loads.append(
            [
                pltpu.make_async_copy(source.at[mat], held.at[mat], in_sem.at[place, mat])
                for place, (source, held) in enumerate(
                    ((orth_ref, orth), (weight_ref, weight), (stored_ref, stored))
                )
            ]
        )
        for copy in loads[-1]:
            copy.start()
    for mat in range(count):
        for copy in loads[mat]:
            copy.wait()
        on = jnp.where(owners_ref[offset + mat] < n_fsdp, jnp.float32(1.0), jnp.float32(0.0))
        held = orth[mat].astype(jnp.float32)
        update[mat] = ((update_scale * on) * held).astype(jnp.bfloat16)
        stepped[mat] = (
            weight[mat].astype(jnp.float32) * (1.0 - (LEARN_RATE * DECAY_RATE) * on)
            - (LEARN_RATE * update_scale * on) * held
        ).astype(jnp.bfloat16)
        for place, (held, target) in enumerate(
            ((stored, momentum_out), (update, update_out), (stepped, weight_out))
        ):
            copy = pltpu.make_async_copy(held.at[mat], target.at[mat], out_sem.at[place, mat])
            copy.start()
            stores.append(copy)
    for copy in stores:
        copy.wait()


def finish(n_fsdp, update_scale, owners, stored, orth, weight):
    count = weight.shape[0]
    anywhere = pl.BlockSpec(memory_space=pl.ANY)
    shape = jax.ShapeDtypeStruct(weight.shape, jnp.bfloat16)
    return pl.pallas_call(
        functools.partial(finish_kernel, n_fsdp, update_scale),
        out_shape=(shape, shape, shape),
        in_specs=[pl.BlockSpec(memory_space=pltpu.SMEM), anywhere, anywhere, anywhere],
        out_specs=(anywhere, anywhere, anywhere),
        scratch_shapes=[pltpu.VMEM(weight.shape, jnp.bfloat16)] * 5
        + [pltpu.SemaphoreType.DMA((3, count))] * 2,
        compiler_params=pltpu.CompilerParams(vmem_limit_bytes=KERNEL_VMEM),
        name="finish",
    )(owners, stored, orth, weight)


def by_collectives(grads, momentum, weight, active, update_scale):
    groups = lax.axis_size("fsdp")
    summed = lax.psum_scatter(
        grads[0], "replica", scatter_dimension=0, tiled=True
    ).astype(jnp.float32)
    local_count, row_count, col_count = momentum.shape
    keep_mask = active[:, None, None]
    old_momentum = momentum.astype(jnp.float32)
    new_momentum = jnp.where(
        keep_mask, MOMENTUM_DECAY * old_momentum + summed, old_momentum
    ).astype(jnp.bfloat16)
    stored = lax.optimization_barrier(new_momentum)
    outgoing = (summed + MOMENTUM_DECAY * stored.astype(jnp.float32)).astype(jnp.bfloat16)
    slots = -(-local_count // groups)
    padding = slots * groups - local_count
    packed = jnp.pad(outgoing, ((0, padding), (0, 0), (0, 0)))
    received = lax.all_to_all(packed, "fsdp", split_axis=0, concat_axis=1, tiled=True)
    orthogonal = newton_blocks(received)
    returned = lax.all_to_all(orthogonal, "fsdp", split_axis=1, concat_axis=0, tiled=True)
    restored = jnp.where(keep_mask, returned[:local_count].astype(jnp.float32), 0.0)
    update = (update_scale * restored).astype(jnp.bfloat16)
    old_weight = weight.astype(jnp.float32)
    stepped = old_weight * (1.0 - LEARN_RATE * DECAY_RATE) - LEARN_RATE * update_scale * restored
    new_weight = jnp.where(keep_mask, stepped, old_weight).astype(jnp.bfloat16)
    return (new_momentum, update, new_weight)


def on_device(grads, momentum, weight, owners):
    n_fsdp = lax.axis_size("fsdp")
    n_rep = lax.axis_size("replica")
    count, row_count, col_count = momentum.shape
    update_scale = UPDATE_RATIO * math.sqrt(max(row_count * n_fsdp, col_count))
    offset = lax.axis_index("replica") * count
    active = lax.dynamic_slice_in_dim(owners, offset, count) < n_fsdp
    held_bytes = 2 * row_count * col_count * (3 * n_rep * count + 4 * count + 8 * n_fsdp)
    fits = held_bytes < KERNEL_VMEM // 2 and row_count % ROW_TILE == 0
    fits = fits and col_count % (128 * PARTS) == 0
    if not fits or n_fsdp % 2 or n_rep < 2 or not 3 <= count <= n_fsdp // 2 + 2:
        return by_collectives(grads, momentum, weight, active, update_scale)
    stored, orth = fused_sum_and_orthogonalize(n_rep, n_fsdp, owners, grads[0], momentum)
    return finish(n_fsdp, update_scale, owners, stored, orth, weight)


def solution(mesh):
    in_specs = (
        P("replica", None, "fsdp", None),
        P("replica", "fsdp", None),
        P("replica", "fsdp", None),
        P(),
    )
    out_specs = (P("replica", "fsdp", None), P("replica", "fsdp", None), P("replica", "fsdp", None))
    return jax.shard_map(
        on_device, mesh=mesh, in_specs=in_specs, out_specs=out_specs, check_vma=False
    )
```

```python
import functools
import math

import jax
import jax.numpy as jnp
from jax import lax
from jax.experimental import pallas as pl
from jax.experimental.pallas import tpu as pltpu
from jax.sharding import PartitionSpec as P

ITERS = 2
ROW_TILE = 8
KERNEL_VMEM = 56 * 1024 * 1024
PARTS = 2
LOOK_AHEAD = 6
GATHER_TURNS = 2


EPSILON = 1e-07
COEFF_LINEAR = 3.4445
COEFF_CUBIC = -4.775
COEFF_QUINTIC = 2.0315
MOMENTUM_DECAY = 0.95
LEARN_RATE = 0.02
DECAY_RATE = 0.1
UPDATE_RATIO = 0.2


def newton_blocks(blocks):
    scaled = blocks.astype(jnp.float32)
    frobenius = jnp.sqrt(jnp.sum(scaled * scaled, axis=(1, 2), keepdims=True))
    iterate = lax.optimization_barrier((scaled / (frobenius + EPSILON)).astype(jnp.bfloat16))
    for turn in range(ITERS):
        gram_matrix = jnp.einsum(
            "cik,cjk->cij", iterate, iterate, preferred_element_type=jnp.float32
        ).astype(jnp.bfloat16)
        gram_matrix = lax.optimization_barrier(gram_matrix)
        gram_square = jnp.einsum(
            "cij,cjk->cik", gram_matrix, gram_matrix, preferred_element_type=jnp.float32
        )
        poly_term = (
            COEFF_CUBIC * gram_matrix.astype(jnp.float32) + COEFF_QUINTIC * gram_square
        ).astype(jnp.bfloat16)
        product = jnp.einsum("cij,cjk->cik", poly_term, iterate, preferred_element_type=jnp.float32)
        iterate = (COEFF_LINEAR * iterate.astype(jnp.float32) + product).astype(jnp.bfloat16)
        iterate = lax.optimization_barrier(iterate)
    return iterate


def add_rows(left, right):
    return left.astype(jnp.float32) + right.astype(jnp.float32)


def fused_kernel(
    n_rep,
    n_fsdp,
    count,
    owners_ref,
    grads_ref,
    momentum_ref,
    stored_out,
    orth_out,
    own,
    old,
    from_left,
    from_right,
    total,
    stored,
    outgoing,
    gathered,
    iterate,
    gram,
    poly,
    finished,
    returned,
    load_sem,
    right_send,
    right_recv,
    left_send,
    left_recv,
    gather_send,
    gather_recv,
    return_send,
    return_recv,
    stored_sem,
    orth_sem,
):
    rep = lax.axis_index("replica")
    me = lax.axis_index("fsdp")
    row_count, col_count = returned.shape[1:]
    width = col_count // PARTS
    units = count * PARTS
    chips = n_fsdp // 2
    early_count = count - 2
    chip, core = me // 2, lax.rem(me, 2)
    partner = me + 1 - 2 * core

    has_early = (core == 1) & (chip < early_count)

    def early_owner(mat):
        return mat * 2 + 1

    def columns(part):
        return pl.ds(pl.multiple_of(part * width, 128), width)

    loads = []
    for part in range(PARTS):
        cols = pl.ds(part * width, width)
        for place, (source, held) in enumerate(((grads_ref, own), (momentum_ref, old))):
            loads.append(
                pltpu.make_async_copy(
                    source.at[:, :, cols], held.at[:, part], load_sem.at[place, part]
                )
            )
            loads[-1].start()

    barrier = pltpu.get_barrier_semaphore()
    for step in range(1, n_fsdp):
        pl.semaphore_signal(barrier, inc=1, device_id={"fsdp": lax.rem(me + step, n_fsdp)})

    @pl.when(rep > 0)
    def _():
        pl.semaphore_signal(barrier, inc=1, device_id={"replica": rep - 1})

    @pl.when(rep < n_rep - 1)
    def _():
        pl.semaphore_signal(barrier, inc=1, device_id={"replica": rep + 1})

    inner = (rep > 0) & (rep < n_rep - 1)
    pl.semaphore_wait(barrier, jnp.where(inner, n_fsdp + 1, n_fsdp))
    for copy in loads:
        copy.wait()

    def right_copy(group, unit, raw=False):
        mat, part = unit // PARTS, lax.rem(unit, PARTS)
        return pltpu.make_async_remote_copy(
            src_ref=own.at[group * count + mat, part] if raw else from_left.at[group, unit],
            dst_ref=from_left.at[group, unit],
            send_sem=right_send.at[group, unit],
            recv_sem=right_recv.at[group, unit],
            device_id={"replica": rep + 1},
        )

    def left_copy(group, unit, raw=False):
        mat, part = unit // PARTS, lax.rem(unit, PARTS)
        return pltpu.make_async_remote_copy(
            src_ref=own.at[group * count + mat, part] if raw else from_right.at[group, unit],
            dst_ref=from_right.at[group, unit],
            send_sem=left_send.at[group, unit],
            recv_sem=left_recv.at[group, unit],
            device_id={"replica": rep - 1},
        )

    def gather_copy(unit, job, slot, target, place):
        part = lax.rem(unit, PARTS)
        return pltpu.make_async_remote_copy(
            src_ref=outgoing.at[unit],
            dst_ref=gathered.at[job, part, slot],
            send_sem=gather_send.at[unit, place],
            recv_sem=gather_recv.at[job, slot, part],
            device_id={"fsdp": target},
        )

    def return_copy(job, mat, slot):
        return pltpu.make_async_remote_copy(
            src_ref=finished.at[job, slot],
            dst_ref=returned.at[mat],
            send_sem=return_send.at[job, slot],
            recv_sem=return_recv.at[mat],
            device_id={"fsdp": slot},
        )

    def stored_copy(unit):
        mat, part = unit // PARTS, lax.rem(unit, PARTS)
        return pltpu.make_async_copy(
            stored.at[unit], stored_out.at[mat, :, columns(part)], stored_sem.at[unit]
        )

    def orth_copy(mat):
        return pltpu.make_async_copy(returned.at[mat], orth_out.at[mat], orth_sem.at[mat])

    def send_raw(unit):
        @pl.when(rep == 0)
        def _():
            for group in range(n_rep - 1, 0, -1):
                right_copy(group, unit, raw=True).start()

        @pl.when(rep == n_rep - 1)
        def _():
            for group in range(n_rep - 1):
                left_copy(group, unit, raw=True).start()

    def forward_right(unit):
        mat, part = unit // PARTS, lax.rem(unit, PARTS)
        for group in range(n_rep - 1, 1, -1):

            @pl.when(rep < group)
            def _():
                right_copy(group, unit).wait_recv()
                from_left[group, unit] = add_rows(
                    from_left[group, unit], own[group * count + mat, part]
                ).astype(jnp.bfloat16)
                right_copy(group, unit).start()

    def forward_left(unit):
        mat, part = unit // PARTS, lax.rem(unit, PARTS)
        for group in range(n_rep - 2):

            @pl.when(rep > group)
            def _():
                left_copy(group, unit).wait_recv()
                from_right[group, unit] = add_rows(
                    from_right[group, unit], own[group * count + mat, part]
                ).astype(jnp.bfloat16)
                left_copy(group, unit).start()

    def each_gather(unit, act):
        mat = unit // PARTS
        late_core = mat - early_count

        @pl.when((mat < early_count) & (me != early_owner(mat)))
        def _():
            act(gather_copy(unit, 0, me, early_owner(mat), 0))

        @pl.when(mat >= early_count)
        def _():
            for step in range(1, chips):
                target = lax.rem(chip + step, chips) * 2 + late_core
                act(gather_copy(unit, 1, me, target, step))

            @pl.when(core != late_core)
            def _():
                act(gather_copy(unit, 1, me, partner, 0))

    def finish_sum(unit):
        mat, part = unit // PARTS, lax.rem(unit, PARTS)
        total[...] = own[rep * count + mat, part].astype(jnp.float32)

        @pl.when(rep > 0)
        def _():
            right_copy(rep, unit).wait_recv()
            total[...] += from_left[rep, unit].astype(jnp.float32)

        @pl.when(rep < n_rep - 1)
        def _():
            left_copy(rep, unit).wait_recv()
            total[...] += from_right[rep, unit].astype(jnp.float32)

        summed = total[...]
        active = owners_ref[rep * count + mat] < n_fsdp
        decay = jnp.where(active, jnp.float32(MOMENTUM_DECAY), jnp.float32(1.0))
        gain = jnp.where(active, jnp.float32(1.0), jnp.float32(0.0))
        kept = (decay * old[mat, part].astype(jnp.float32) + gain * summed).astype(jnp.bfloat16)
        stored[unit] = kept
        stored_copy(unit).start()
        nesterov = (summed + MOMENTUM_DECAY * kept.astype(jnp.float32)).astype(jnp.bfloat16)
        outgoing[unit] = nesterov

        @pl.when((mat < early_count) & (me == early_owner(mat)))
        def _():
            gathered[0, part, me] = nesterov

        @pl.when((mat >= early_count) & (core == mat - early_count))
        def _():
            gathered[1, part, me] = nesterov

        each_gather(unit, lambda copy: copy.start())

    def make_gram():
        held = iterate[...]
        gram[...] = lax.dot_general(
            held, held, (((1,), (1,)), ((), ())), preferred_element_type=jnp.float32
        ).astype(jnp.bfloat16)

    def make_poly(rows):
        square = jnp.dot(gram[rows, :], gram[...], preferred_element_type=jnp.float32)
        poly[rows, :] = (
            COEFF_CUBIC * gram[rows, :].astype(jnp.float32) + COEFF_QUINTIC * square
        ).astype(jnp.bfloat16)

    def apply_poly(rows):
        product = jnp.dot(poly[rows, :], iterate[...], preferred_element_type=jnp.float32)
        return COEFF_LINEAR * iterate[rows, :].astype(jnp.float32) + product

    def orthogonalize(job, mat):
        @pl.loop(1, n_fsdp)
        def _(step):
            for part in range(PARTS):
                unit = mat * PARTS + part
                gather_copy(unit, job, lax.rem(me + step, n_fsdp), me, 0).wait_recv()

        scaled = gathered[job].astype(jnp.float32)
        frobenius = jnp.sqrt(jnp.sum(scaled * scaled))
        inverse = 1.0 / (frobenius + EPSILON)
        for part in range(PARTS):
            iterate[:, pl.ds(part * width, width)] = (
                (scaled[part] * inverse).reshape(n_fsdp * row_count, width).astype(jnp.bfloat16)
            )
        whole = pl.ds(0, n_fsdp * row_count)
        for turn in range(ITERS - 1):
            make_gram()
            make_poly(whole)
            iterate[...] = apply_poly(whole).astype(jnp.bfloat16)
        make_gram()

        @pl.when(job == 0)
        def _():
            make_poly(whole)
            finished[0] = (
                apply_poly(whole).reshape(n_fsdp, row_count, col_count).astype(jnp.bfloat16)
            )

            @pl.loop(1, n_fsdp)
            def _(step):
                return_copy(0, mat, lax.rem(me + step, n_fsdp)).start()

            returned[mat] = finished[0, me]

        @pl.when(job == 1)
        def _():
            pair = pl.ds(pl.multiple_of(chip * (2 * row_count), 16), 2 * row_count)
            make_poly(pair)
            rows = apply_poly(pair).reshape(2, row_count, col_count).astype(jnp.bfloat16)
            finished[1, pl.ds(chip * 2, 2)] = rows
            return_copy(1, mat, partner).start()
            returned[mat] = finished[1, me]

    ahead = min(LOOK_AHEAD, units)
    for unit in range(ahead):
        send_raw(unit)

    right_lag, left_lag = rep - 1, n_rep - 2 - rep
    sum_lag = jnp.maximum(right_lag, left_lag)

    @pl.loop(0, units + n_rep - 2)
    def _(turn):
        @pl.when(turn < units - ahead)
        def _():
            send_raw(turn + ahead)

        to_right, to_left, to_sum = turn - right_lag, turn - left_lag, turn - sum_lag

        @pl.when((rep > 0) & (to_right >= 0) & (to_right < units))
        def _():
            forward_right(to_right)

        @pl.when((rep < n_rep - 1) & (to_left >= 0) & (to_left < units))
        def _():
            forward_left(to_left)

        @pl.when((to_sum >= 0) & (to_sum < units))
        def _():
            finish_sum(to_sum)

        last = to_sum == units - 1
        early = has_early & (to_sum == (chip + 1) * PARTS - 1 + GATHER_TURNS)

        @pl.when(last | early)
        def _():
            job = jnp.where(last, 1, 0)
            orthogonalize(job, jnp.where(last, early_count + core, chip))

    @pl.loop(0, count)
    def _(mat):
        held_here = jnp.where(
            mat < early_count, me == early_owner(mat), core == mat - early_count
        )

        @pl.when(jnp.logical_not(held_here))
        def _():
            return_copy(0, mat, me).wait_recv()

        orth_copy(mat).start()

    @pl.loop(0, units)
    def _(unit):
        for group in range(n_rep):

            @pl.when(rep < group)
            def _():
                right_copy(group, unit).wait_send()

            @pl.when(rep > group)
            def _():
                left_copy(group, unit).wait_send()

        each_gather(unit, lambda copy: copy.wait_send())
        stored_copy(unit).wait()

    @pl.loop(0, count)
    def _(mat):
        orth_copy(mat).wait()

    @pl.when(has_early)
    def _():
        @pl.loop(1, n_fsdp)
        def _(step):
            return_copy(0, chip, lax.rem(me + step, n_fsdp)).wait_send()

    return_copy(1, early_count + core, partner).wait_send()


def fused_sum_and_orthogonalize(n_rep, n_fsdp, owners, grads, momentum):
    count, row_count, col_count = momentum.shape
    all_rows = n_fsdp * row_count
    units = count * PARTS
    block = (row_count, col_count)
    piece = (row_count, col_count // PARTS)
    half = jnp.bfloat16
    shape = jax.ShapeDtypeStruct(momentum.shape, half)
    dma = pltpu.SemaphoreType.DMA
    return pl.pallas_call(
        functools.partial(fused_kernel, n_rep, n_fsdp, count),
        out_shape=(shape, shape),
        in_specs=[
            pl.BlockSpec(memory_space=pltpu.SMEM),
            pl.BlockSpec(memory_space=pl.ANY),
            pl.BlockSpec(memory_space=pl.ANY),
        ],
        out_specs=(pl.BlockSpec(memory_space=pl.ANY), pl.BlockSpec(memory_space=pl.ANY)),
        scratch_shapes=[
            pltpu.VMEM((n_rep * count, PARTS, *piece), half),
            pltpu.VMEM((count, PARTS, *piece), half),
            pltpu.VMEM((n_rep, units, *piece), half),
            pltpu.VMEM((n_rep, units, *piece), half),
            pltpu.VMEM(piece, jnp.float32),
            pltpu.VMEM((units, *piece), half),
            pltpu.VMEM((units, *piece), half),
            pltpu.VMEM((2, PARTS, n_fsdp, *piece), half),
            pltpu.VMEM((all_rows, col_count), half),
            pltpu.VMEM((all_rows, all_rows), half),
            pltpu.VMEM((all_rows, all_rows), half),
            pltpu.VMEM((2, n_fsdp, *block), half),
            pltpu.VMEM((count, *block), half),
            dma((2, PARTS)),
            dma((n_rep, units)),
            dma((n_rep, units)),
            dma((n_rep, units)),
            dma((n_rep, units)),
            dma((units, n_fsdp // 2)),
            dma((2, n_fsdp, PARTS)),
            dma((2, n_fsdp)),
            dma((count,)),
            dma((units,)),
            dma((count,)),
        ],
        compiler_params=pltpu.CompilerParams(
            collective_id=0, has_side_effects=True, vmem_limit_bytes=KERNEL_VMEM
        ),
        name="sum_and_orthogonalize",
    )(owners, grads, momentum)


def finish_kernel(
    n_fsdp,
    update_scale,
    owners_ref,
    stored_ref,
    orth_ref,
    weight_ref,
    momentum_out,
    update_out,
    weight_out,
    stored,
    orth,
    weight,
    update,
    stepped,
    in_sem,
    out_sem,
):
    count = weight_ref.shape[0]
    offset = lax.axis_index("replica") * count
    loads, stores = [], []
    for mat in range(count):
        loads.append(
            [
                pltpu.make_async_copy(source.at[mat], held.at[mat], in_sem.at[place, mat])
                for place, (source, held) in enumerate(
                    ((orth_ref, orth), (weight_ref, weight), (stored_ref, stored))
                )
            ]
        )
        for copy in loads[-1]:
            copy.start()
    for mat in range(count):
        for copy in loads[mat]:
            copy.wait()
        on = jnp.where(owners_ref[offset + mat] < n_fsdp, jnp.float32(1.0), jnp.float32(0.0))
        held = orth[mat].astype(jnp.float32)
        update[mat] = ((update_scale * on) * held).astype(jnp.bfloat16)
        stepped[mat] = (
            weight[mat].astype(jnp.float32) * (1.0 - (LEARN_RATE * DECAY_RATE) * on)
            - (LEARN_RATE * update_scale * on) * held
        ).astype(jnp.bfloat16)
        for place, (held, target) in enumerate(
            ((stored, momentum_out), (update, update_out), (stepped, weight_out))
        ):
            copy = pltpu.make_async_copy(held.at[mat], target.at[mat], out_sem.at[place, mat])
            copy.start()
            stores.append(copy)
    for copy in stores:
        copy.wait()


def finish(n_fsdp, update_scale, owners, stored, orth, weight):
    count = weight.shape[0]
    anywhere = pl.BlockSpec(memory_space=pl.ANY)
    shape = jax.ShapeDtypeStruct(weight.shape, jnp.bfloat16)
    return pl.pallas_call(
        functools.partial(finish_kernel, n_fsdp, update_scale),
        out_shape=(shape, shape, shape),
        in_specs=[pl.BlockSpec(memory_space=pltpu.SMEM), anywhere, anywhere, anywhere],
        out_specs=(anywhere, anywhere, anywhere),
        scratch_shapes=[pltpu.VMEM(weight.shape, jnp.bfloat16)] * 5
        + [pltpu.SemaphoreType.DMA((3, count))] * 2,
        compiler_params=pltpu.CompilerParams(vmem_limit_bytes=KERNEL_VMEM),
        name="finish",
    )(owners, stored, orth, weight)


def by_collectives(grads, momentum, weight, active, update_scale):
    groups = lax.axis_size("fsdp")
    summed = lax.psum_scatter(
        grads[0], "replica", scatter_dimension=0, tiled=True
    ).astype(jnp.float32)
    local_count, row_count, col_count = momentum.shape
    keep_mask = active[:, None, None]
    old_momentum = momentum.astype(jnp.float32)
    new_momentum = jnp.where(
        keep_mask, MOMENTUM_DECAY * old_momentum + summed, old_momentum
    ).astype(jnp.bfloat16)
    stored = lax.optimization_barrier(new_momentum)
    outgoing = (summed + MOMENTUM_DECAY * stored.astype(jnp.float32)).astype(jnp.bfloat16)
    slots = -(-local_count // groups)
    padding = slots * groups - local_count
    packed = jnp.pad(outgoing, ((0, padding), (0, 0), (0, 0)))
    received = lax.all_to_all(packed, "fsdp", split_axis=0, concat_axis=1, tiled=True)
    orthogonal = newton_blocks(received)
    returned = lax.all_to_all(orthogonal, "fsdp", split_axis=1, concat_axis=0, tiled=True)
    restored = jnp.where(keep_mask, returned[:local_count].astype(jnp.float32), 0.0)
    update = (update_scale * restored).astype(jnp.bfloat16)
    old_weight = weight.astype(jnp.float32)
    stepped = old_weight * (1.0 - LEARN_RATE * DECAY_RATE) - LEARN_RATE * update_scale * restored
    new_weight = jnp.where(keep_mask, stepped, old_weight).astype(jnp.bfloat16)
    return (new_momentum, update, new_weight)


def on_device(grads, momentum, weight, owners):
    n_fsdp = lax.axis_size("fsdp")
    n_rep = lax.axis_size("replica")
    count, row_count, col_count = momentum.shape
    update_scale = UPDATE_RATIO * math.sqrt(max(row_count * n_fsdp, col_count))
    offset = lax.axis_index("replica") * count
    active = lax.dynamic_slice_in_dim(owners, offset, count) < n_fsdp
    held_bytes = 2 * row_count * col_count * (3 * n_rep * count + 4 * count + 8 * n_fsdp)
    fits = held_bytes < KERNEL_VMEM // 2 and row_count % ROW_TILE == 0
    fits = fits and col_count % (128 * PARTS) == 0
    if not fits or n_fsdp % 2 or n_rep < 2 or not 3 <= count <= n_fsdp // 2 + 2:
        return by_collectives(grads, momentum, weight, active, update_scale)
    stored, orth = fused_sum_and_orthogonalize(n_rep, n_fsdp, owners, grads[0], momentum)
    return finish(n_fsdp, update_scale, owners, stored, orth, weight)


def solution(mesh):
    in_specs = (
        P("replica", None, "fsdp", None),
        P("replica", "fsdp", None),
        P("replica", "fsdp", None),
        P(),
    )
    out_specs = (P("replica", "fsdp", None), P("replica", "fsdp", None), P("replica", "fsdp", None))
    return jax.shard_map(
        on_device, mesh=mesh, in_specs=in_specs, out_specs=out_specs, check_vma=False
    )
```

```python
import functools
import math

import jax
import jax.numpy as jnp
from jax import lax
from jax.experimental import pallas as pl
from jax.experimental.pallas import tpu as pltpu
from jax.sharding import PartitionSpec as P

ITERS = 2
ROW_TILE = 8
KERNEL_VMEM = 56 * 1024 * 1024
PARTS = 2
LOOK_AHEAD = 6
GATHER_TURNS = 2


EPSILON = 1e-07
COEFF_LINEAR = 3.4445
COEFF_CUBIC = -4.775
COEFF_QUINTIC = 2.0315
MOMENTUM_DECAY = 0.95
LEARN_RATE = 0.02
DECAY_RATE = 0.1
UPDATE_RATIO = 0.2


def newton_blocks(blocks):
    scaled = blocks.astype(jnp.float32)
    frobenius = jnp.sqrt(jnp.sum(scaled * scaled, axis=(1, 2), keepdims=True))
    iterate = lax.optimization_barrier((scaled / (frobenius + EPSILON)).astype(jnp.bfloat16))
    for turn in range(ITERS):
        gram_matrix = jnp.einsum(
            "cik,cjk->cij", iterate, iterate, preferred_element_type=jnp.float32
        ).astype(jnp.bfloat16)
        gram_matrix = lax.optimization_barrier(gram_matrix)
        gram_square = jnp.einsum(
            "cij,cjk->cik", gram_matrix, gram_matrix, preferred_element_type=jnp.float32
        )
        poly_term = (
            COEFF_CUBIC * gram_matrix.astype(jnp.float32) + COEFF_QUINTIC * gram_square
        ).astype(jnp.bfloat16)
        product = jnp.einsum("cij,cjk->cik", poly_term, iterate, preferred_element_type=jnp.float32)
        iterate = (COEFF_LINEAR * iterate.astype(jnp.float32) + product).astype(jnp.bfloat16)
        iterate = lax.optimization_barrier(iterate)
    return iterate


def add_rows(left, right):
    return left.astype(jnp.float32) + right.astype(jnp.float32)


def fused_kernel(
    n_rep,
    n_fsdp,
    count,
    owners_ref,
    grads_ref,
    momentum_ref,
    stored_out,
    orth_out,
    own,
    old,
    from_left,
    from_right,
    total,
    stored,
    outgoing,
    gathered,
    iterate,
    gram,
    poly,
    finished,
    returned,
    load_sem,
    right_send,
    right_recv,
    left_send,
    left_recv,
    gather_send,
    gather_recv,
    return_send,
    return_recv,
    stored_sem,
    orth_sem,
):
    rep = lax.axis_index("replica")
    me = lax.axis_index("fsdp")
    row_count, col_count = returned.shape[1:]
    width = col_count // PARTS
    units = count * PARTS
    chips = n_fsdp // 2
    chip, core = me // 2, lax.rem(me, 2)
    partner = me + 1 - 2 * core

    def columns(part):
        return pl.ds(pl.multiple_of(part * width, 128), width)

    loads = []
    for part in range(PARTS):
        cols = pl.ds(part * width, width)
        for place, (source, held) in enumerate(((grads_ref, own), (momentum_ref, old))):
            loads.append(
                pltpu.make_async_copy(
                    source.at[:, :, cols], held.at[:, part], load_sem.at[place, part]
                )
            )
            loads[-1].start()

    barrier = pltpu.get_barrier_semaphore()
    for step in range(1, n_fsdp):
        pl.semaphore_signal(barrier, inc=1, device_id={"fsdp": lax.rem(me + step, n_fsdp)})

    @pl.when(rep > 0)
    def _():
        pl.semaphore_signal(barrier, inc=1, device_id={"replica": rep - 1})

    @pl.when(rep < n_rep - 1)
    def _():
        pl.semaphore_signal(barrier, inc=1, device_id={"replica": rep + 1})

    inner = (rep > 0) & (rep < n_rep - 1)
    pl.semaphore_wait(barrier, jnp.where(inner, n_fsdp + 1, n_fsdp))
    for copy in loads:
        copy.wait()

    def right_copy(group, unit, raw=False):
        mat, part = unit // PARTS, lax.rem(unit, PARTS)
        return pltpu.make_async_remote_copy(
            src_ref=own.at[group * count + mat, part] if raw else from_left.at[group, unit],
            dst_ref=from_left.at[group, unit],
            send_sem=right_send.at[group, unit],
            recv_sem=right_recv.at[group, unit],
            device_id={"replica": rep + 1},
        )

    def left_copy(group, unit, raw=False):
        mat, part = unit // PARTS, lax.rem(unit, PARTS)
        return pltpu.make_async_remote_copy(
            src_ref=own.at[group * count + mat, part] if raw else from_right.at[group, unit],
            dst_ref=from_right.at[group, unit],
            send_sem=left_send.at[group, unit],
            recv_sem=left_recv.at[group, unit],
            device_id={"replica": rep - 1},
        )

    def gather_copy(unit, slot, target, place):
        mat, part = unit // PARTS, lax.rem(unit, PARTS)
        return pltpu.make_async_remote_copy(
            src_ref=outgoing.at[unit],
            dst_ref=gathered.at[mat // 2, part, slot],
            send_sem=gather_send.at[unit, place],
            recv_sem=gather_recv.at[mat // 2, slot, part],
            device_id={"fsdp": target},
        )

    def return_copy(mat):
        return pltpu.make_async_remote_copy(
            src_ref=finished.at[mat // 2],
            dst_ref=returned.at[mat],
            send_sem=return_send.at[mat // 2],
            recv_sem=return_recv.at[mat],
            device_id={"fsdp": partner},
        )

    def stored_copy(unit):
        mat, part = unit // PARTS, lax.rem(unit, PARTS)
        return pltpu.make_async_copy(
            stored.at[unit], stored_out.at[mat, :, columns(part)], stored_sem.at[unit]
        )

    def orth_copy(mat):
        return pltpu.make_async_copy(returned.at[mat], orth_out.at[mat], orth_sem.at[mat])

    def send_raw(unit):
        @pl.when(rep == 0)
        def _():
            for group in range(n_rep - 1, 0, -1):
                right_copy(group, unit, raw=True).start()

        @pl.when(rep == n_rep - 1)
        def _():
            for group in range(n_rep - 1):
                left_copy(group, unit, raw=True).start()

    def forward_right(unit):
        mat, part = unit // PARTS, lax.rem(unit, PARTS)
        for group in range(n_rep - 1, 1, -1):

            @pl.when(rep < group)
            def _():
                right_copy(group, unit).wait_recv()
                from_left[group, unit] = add_rows(
                    from_left[group, unit], own[group * count + mat, part]
                ).astype(jnp.bfloat16)
                right_copy(group, unit).start()

    def forward_left(unit):
        mat, part = unit // PARTS, lax.rem(unit, PARTS)
        for group in range(n_rep - 2):

            @pl.when(rep > group)
            def _():
                left_copy(group, unit).wait_recv()
                from_right[group, unit] = add_rows(
                    from_right[group, unit], own[group * count + mat, part]
                ).astype(jnp.bfloat16)
                left_copy(group, unit).start()

    def each_gather(unit, act):
        solver = lax.rem(unit // PARTS, 2)
        for step in range(1, chips):
            act(gather_copy(unit, me, lax.rem(chip + step, chips) * 2 + solver, step))

        @pl.when(core != solver)
        def _():
            act(gather_copy(unit, me, partner, 0))

    def finish_sum(unit):
        mat, part = unit // PARTS, lax.rem(unit, PARTS)
        total[...] = own[rep * count + mat, part].astype(jnp.float32)

        @pl.when(rep > 0)
        def _():
            right_copy(rep, unit).wait_recv()
            total[...] += from_left[rep, unit].astype(jnp.float32)

        @pl.when(rep < n_rep - 1)
        def _():
            left_copy(rep, unit).wait_recv()
            total[...] += from_right[rep, unit].astype(jnp.float32)

        summed = total[...]
        active = owners_ref[rep * count + mat] < n_fsdp
        decay = jnp.where(active, jnp.float32(MOMENTUM_DECAY), jnp.float32(1.0))
        gain = jnp.where(active, jnp.float32(1.0), jnp.float32(0.0))
        kept = (decay * old[mat, part].astype(jnp.float32) + gain * summed).astype(jnp.bfloat16)
        stored[unit] = kept
        stored_copy(unit).start()
        nesterov = (summed + MOMENTUM_DECAY * kept.astype(jnp.float32)).astype(jnp.bfloat16)
        outgoing[unit] = nesterov

        @pl.when(core == lax.rem(mat, 2))
        def _():
            gathered[mat // 2, part, me] = nesterov

        each_gather(unit, lambda copy: copy.start())

    def make_gram():
        held = iterate[...]
        gram[...] = lax.dot_general(
            held, held, (((1,), (1,)), ((), ())), preferred_element_type=jnp.float32
        ).astype(jnp.bfloat16)

    def make_poly(rows):
        square = jnp.dot(gram[rows, :], gram[...], preferred_element_type=jnp.float32)
        poly[rows, :] = (
            COEFF_CUBIC * gram[rows, :].astype(jnp.float32) + COEFF_QUINTIC * square
        ).astype(jnp.bfloat16)

    def apply_poly(rows):
        product = jnp.dot(poly[rows, :], iterate[...], preferred_element_type=jnp.float32)
        return COEFF_LINEAR * iterate[rows, :].astype(jnp.float32) + product

    whole = pl.ds(0, n_fsdp * row_count)

    def normalize(mat):
        @pl.loop(1, n_fsdp)
        def _(step):
            for part in range(PARTS):
                gather_copy(mat * PARTS + part, lax.rem(me + step, n_fsdp), me, 0).wait_recv()

        scaled = gathered[mat // 2].astype(jnp.float32)
        frobenius = jnp.sqrt(jnp.sum(scaled * scaled))
        inverse = 1.0 / (frobenius + EPSILON)
        for part in range(PARTS):
            iterate[:, pl.ds(part * width, width)] = (
                (scaled[part] * inverse).reshape(n_fsdp * row_count, width).astype(jnp.bfloat16)
            )
        make_gram()

    def iterate_once():
        make_poly(whole)
        iterate[...] = apply_poly(whole).astype(jnp.bfloat16)

    def last_iterate(mat):
        make_gram()
        pair = pl.ds(pl.multiple_of(chip * (2 * row_count), 16), 2 * row_count)
        make_poly(pair)
        rows = apply_poly(pair).reshape(2, row_count, col_count).astype(jnp.bfloat16)
        for side in range(2):

            @pl.when(core == side)
            def _():
                returned[mat] = rows[side]
                finished[mat // 2] = rows[1 - side]

        return_copy(mat).start()

    ahead = min(LOOK_AHEAD, units)
    for unit in range(ahead):
        send_raw(unit)

    right_lag, left_lag = rep - 1, n_rep - 2 - rep
    sum_lag = jnp.maximum(right_lag, left_lag)

    @pl.loop(0, units + GATHER_TURNS + 2 + n_rep - 2)
    def _(turn):
        @pl.when(turn < units - ahead)
        def _():
            send_raw(turn + ahead)

        to_right, to_left, to_sum = turn - right_lag, turn - left_lag, turn - sum_lag

        @pl.when((rep > 0) & (to_right >= 0) & (to_right < units))
        def _():
            forward_right(to_right)

        @pl.when((rep < n_rep - 1) & (to_left >= 0) & (to_left < units))
        def _():
            forward_left(to_left)

        @pl.when((to_sum >= 0) & (to_sum < units))
        def _():
            finish_sum(to_sum)

        place = to_sum - GATHER_TURNS - (core + 1) * PARTS + 1
        mat = place // (2 * PARTS) * 2 + core
        stage = lax.rem(place, 2 * PARTS)
        ready = (place >= 0) & (mat < count)

        @pl.when(ready & (stage == 0))
        def _():
            normalize(mat)

        @pl.when(ready & (stage == 1))
        def _():
            iterate_once()

        @pl.when(ready & (stage == 2))
        def _():
            last_iterate(mat)

    @pl.loop(0, count)
    def _(mat):
        @pl.when(core != lax.rem(mat, 2))
        def _():
            return_copy(mat).wait_recv()

        orth_copy(mat).start()

    @pl.loop(0, units)
    def _(unit):
        for group in range(n_rep):

            @pl.when(rep < group)
            def _():
                right_copy(group, unit).wait_send()

            @pl.when(rep > group)
            def _():
                left_copy(group, unit).wait_send()

        each_gather(unit, lambda copy: copy.wait_send())
        stored_copy(unit).wait()

    @pl.loop(0, count)
    def _(mat):
        orth_copy(mat).wait()

    @pl.loop(0, count)
    def _(mat):
        @pl.when(core == lax.rem(mat, 2))
        def _():
            return_copy(mat).wait_send()


def fused_sum_and_orthogonalize(n_rep, n_fsdp, owners, grads, momentum):
    count, row_count, col_count = momentum.shape
    all_rows = n_fsdp * row_count
    units = count * PARTS
    jobs = (count + 1) // 2
    block = (row_count, col_count)
    piece = (row_count, col_count // PARTS)
    half = jnp.bfloat16
    shape = jax.ShapeDtypeStruct(momentum.shape, half)
    dma = pltpu.SemaphoreType.DMA
    return pl.pallas_call(
        functools.partial(fused_kernel, n_rep, n_fsdp, count),
        out_shape=(shape, shape),
        in_specs=[
            pl.BlockSpec(memory_space=pltpu.SMEM),
            pl.BlockSpec(memory_space=pl.ANY),
            pl.BlockSpec(memory_space=pl.ANY),
        ],
        out_specs=(pl.BlockSpec(memory_space=pl.ANY), pl.BlockSpec(memory_space=pl.ANY)),
        scratch_shapes=[
            pltpu.VMEM((n_rep * count, PARTS, *piece), half),
            pltpu.VMEM((count, PARTS, *piece), half),
            pltpu.VMEM((n_rep, units, *piece), half),
            pltpu.VMEM((n_rep, units, *piece), half),
            pltpu.VMEM(piece, jnp.float32),
            pltpu.VMEM((units, *piece), half),
            pltpu.VMEM((units, *piece), half),
            pltpu.VMEM((jobs, PARTS, n_fsdp, *piece), half),
            pltpu.VMEM((all_rows, col_count), half),
            pltpu.VMEM((all_rows, all_rows), half),
            pltpu.VMEM((all_rows, all_rows), half),
            pltpu.VMEM((jobs, *block), half),
            pltpu.VMEM((count, *block), half),
            dma((2, PARTS)),
            dma((n_rep, units)),
            dma((n_rep, units)),
            dma((n_rep, units)),
            dma((n_rep, units)),
            dma((units, n_fsdp // 2)),
            dma((jobs, n_fsdp, PARTS)),
            dma((jobs,)),
            dma((count,)),
            dma((units,)),
            dma((count,)),
        ],
        compiler_params=pltpu.CompilerParams(
            collective_id=0, has_side_effects=True, vmem_limit_bytes=KERNEL_VMEM
        ),
        name="sum_and_orthogonalize",
    )(owners, grads, momentum)


def finish_kernel(
    n_fsdp,
    update_scale,
    owners_ref,
    stored_ref,
    orth_ref,
    weight_ref,
    momentum_out,
    update_out,
    weight_out,
    stored,
    orth,
    weight,
    update,
    stepped,
    in_sem,
    out_sem,
):
    count = weight_ref.shape[0]
    offset = lax.axis_index("replica") * count
    loads, stores = [], []
    for mat in range(count):
        loads.append(
            [
                pltpu.make_async_copy(source.at[mat], held.at[mat], in_sem.at[place, mat])
                for place, (source, held) in enumerate(
                    ((orth_ref, orth), (weight_ref, weight), (stored_ref, stored))
                )
            ]
        )
        for copy in loads[-1]:
            copy.start()
    for mat in range(count):
        for copy in loads[mat]:
            copy.wait()
        on = jnp.where(owners_ref[offset + mat] < n_fsdp, jnp.float32(1.0), jnp.float32(0.0))
        held = orth[mat].astype(jnp.float32)
        update[mat] = ((update_scale * on) * held).astype(jnp.bfloat16)
        stepped[mat] = (
            weight[mat].astype(jnp.float32) * (1.0 - (LEARN_RATE * DECAY_RATE) * on)
            - (LEARN_RATE * update_scale * on) * held
        ).astype(jnp.bfloat16)
        for place, (held, target) in enumerate(
            ((stored, momentum_out), (update, update_out), (stepped, weight_out))
        ):
            copy = pltpu.make_async_copy(held.at[mat], target.at[mat], out_sem.at[place, mat])
            copy.start()
            stores.append(copy)
    for copy in stores:
        copy.wait()


def finish(n_fsdp, update_scale, owners, stored, orth, weight):
    count = weight.shape[0]
    anywhere = pl.BlockSpec(memory_space=pl.ANY)
    shape = jax.ShapeDtypeStruct(weight.shape, jnp.bfloat16)
    return pl.pallas_call(
        functools.partial(finish_kernel, n_fsdp, update_scale),
        out_shape=(shape, shape, shape),
        in_specs=[pl.BlockSpec(memory_space=pltpu.SMEM), anywhere, anywhere, anywhere],
        out_specs=(anywhere, anywhere, anywhere),
        scratch_shapes=[pltpu.VMEM(weight.shape, jnp.bfloat16)] * 5
        + [pltpu.SemaphoreType.DMA((3, count))] * 2,
        compiler_params=pltpu.CompilerParams(vmem_limit_bytes=KERNEL_VMEM),
        name="finish",
    )(owners, stored, orth, weight)


def by_collectives(grads, momentum, weight, active, update_scale):
    groups = lax.axis_size("fsdp")
    summed = lax.psum_scatter(
        grads[0], "replica", scatter_dimension=0, tiled=True
    ).astype(jnp.float32)
    local_count, row_count, col_count = momentum.shape
    keep_mask = active[:, None, None]
    old_momentum = momentum.astype(jnp.float32)
    new_momentum = jnp.where(
        keep_mask, MOMENTUM_DECAY * old_momentum + summed, old_momentum
    ).astype(jnp.bfloat16)
    stored = lax.optimization_barrier(new_momentum)
    outgoing = (summed + MOMENTUM_DECAY * stored.astype(jnp.float32)).astype(jnp.bfloat16)
    slots = -(-local_count // groups)
    padding = slots * groups - local_count
    packed = jnp.pad(outgoing, ((0, padding), (0, 0), (0, 0)))
    received = lax.all_to_all(packed, "fsdp", split_axis=0, concat_axis=1, tiled=True)
    orthogonal = newton_blocks(received)
    returned = lax.all_to_all(orthogonal, "fsdp", split_axis=1, concat_axis=0, tiled=True)
    restored = jnp.where(keep_mask, returned[:local_count].astype(jnp.float32), 0.0)
    update = (update_scale * restored).astype(jnp.bfloat16)
    old_weight = weight.astype(jnp.float32)
    stepped = old_weight * (1.0 - LEARN_RATE * DECAY_RATE) - LEARN_RATE * update_scale * restored
    new_weight = jnp.where(keep_mask, stepped, old_weight).astype(jnp.bfloat16)
    return (new_momentum, update, new_weight)


def on_device(grads, momentum, weight, owners):
    n_fsdp = lax.axis_size("fsdp")
    n_rep = lax.axis_size("replica")
    count, row_count, col_count = momentum.shape
    update_scale = UPDATE_RATIO * math.sqrt(max(row_count * n_fsdp, col_count))
    offset = lax.axis_index("replica") * count
    active = lax.dynamic_slice_in_dim(owners, offset, count) < n_fsdp
    held_bytes = 2 * row_count * col_count * (3 * n_rep * count + 5 * count + (count + 5) * n_fsdp // 2)
    fits = held_bytes < KERNEL_VMEM // 2 and row_count % ROW_TILE == 0
    fits = fits and col_count % (128 * PARTS) == 0
    if not fits or n_fsdp % 2 or n_rep < 2:
        return by_collectives(grads, momentum, weight, active, update_scale)
    stored, orth = fused_sum_and_orthogonalize(n_rep, n_fsdp, owners, grads[0], momentum)
    return finish(n_fsdp, update_scale, owners, stored, orth, weight)


def solution(mesh):
    in_specs = (
        P("replica", None, "fsdp", None),
        P("replica", "fsdp", None),
        P("replica", "fsdp", None),
        P(),
    )
    out_specs = (P("replica", "fsdp", None), P("replica", "fsdp", None), P("replica", "fsdp", None))
    return jax.shard_map(
        on_device, mesh=mesh, in_specs=in_specs, out_specs=out_specs, check_vma=False
    )
```

```python
import functools
import math

import jax
import jax.numpy as jnp
from jax import lax
from jax.experimental import pallas as pl
from jax.experimental.pallas import tpu as pltpu
from jax.sharding import PartitionSpec as P

ITERS = 2
ROW_TILE = 8
KERNEL_VMEM = 56 * 1024 * 1024
PARTS = 2
GRAM_TILE = 256
LOOK_AHEAD = 6
GATHER_TURNS = 2


EPSILON = 1e-07
COEFF_LINEAR = 3.4445
COEFF_CUBIC = -4.775
COEFF_QUINTIC = 2.0315
MOMENTUM_DECAY = 0.95
LEARN_RATE = 0.02
DECAY_RATE = 0.1
UPDATE_RATIO = 0.2


def newton_blocks(blocks):
    scaled = blocks.astype(jnp.float32)
    frobenius = jnp.sqrt(jnp.sum(scaled * scaled, axis=(1, 2), keepdims=True))
    iterate = lax.optimization_barrier((scaled / (frobenius + EPSILON)).astype(jnp.bfloat16))
    for turn in range(ITERS):
        gram_matrix = jnp.einsum(
            "cik,cjk->cij", iterate, iterate, preferred_element_type=jnp.float32
        ).astype(jnp.bfloat16)
        gram_matrix = lax.optimization_barrier(gram_matrix)
        gram_square = jnp.einsum(
            "cij,cjk->cik", gram_matrix, gram_matrix, preferred_element_type=jnp.float32
        )
        poly_term = (
            COEFF_CUBIC * gram_matrix.astype(jnp.float32) + COEFF_QUINTIC * gram_square
        ).astype(jnp.bfloat16)
        product = jnp.einsum("cij,cjk->cik", poly_term, iterate, preferred_element_type=jnp.float32)
        iterate = (COEFF_LINEAR * iterate.astype(jnp.float32) + product).astype(jnp.bfloat16)
        iterate = lax.optimization_barrier(iterate)
    return iterate


def add_rows(left, right):
    return left.astype(jnp.float32) + right.astype(jnp.float32)


def fused_kernel(
    n_rep,
    n_fsdp,
    count,
    owners_ref,
    grads_ref,
    momentum_ref,
    stored_out,
    orth_out,
    own,
    old,
    from_left,
    from_right,
    total,
    stored,
    outgoing,
    gathered,
    iterate,
    gram,
    poly,
    finished,
    returned,
    load_sem,
    right_send,
    right_recv,
    left_send,
    left_recv,
    gather_send,
    gather_recv,
    return_send,
    return_recv,
    stored_sem,
    orth_sem,
):
    rep = lax.axis_index("replica")
    me = lax.axis_index("fsdp")
    row_count, col_count = returned.shape[1:]
    width = col_count // PARTS
    units = count * PARTS
    chips = n_fsdp // 2
    chip, core = me // 2, lax.rem(me, 2)
    partner = me + 1 - 2 * core

    def columns(part):
        return pl.ds(pl.multiple_of(part * width, 128), width)

    loads = []
    for place, (source, held) in enumerate(((grads_ref, own), (momentum_ref, old))):
        for part in range(PARTS):
            cols = pl.ds(part * width, width)
            loads.append(
                pltpu.make_async_copy(
                    source.at[:, :, cols], held.at[:, part], load_sem.at[place, part]
                )
            )
            loads[-1].start()

    barrier = pltpu.get_barrier_semaphore()
    for step in range(1, n_fsdp):
        pl.semaphore_signal(barrier, inc=1, device_id={"fsdp": lax.rem(me + step, n_fsdp)})

    @pl.when(rep > 0)
    def _():
        pl.semaphore_signal(barrier, inc=1, device_id={"replica": rep - 1})

    @pl.when(rep < n_rep - 1)
    def _():
        pl.semaphore_signal(barrier, inc=1, device_id={"replica": rep + 1})

    inner = (rep > 0) & (rep < n_rep - 1)
    pl.semaphore_wait(barrier, jnp.where(inner, n_fsdp + 1, n_fsdp))
    loads[0].wait()

    def right_copy(group, unit, raw=False):
        mat, part = unit // PARTS, lax.rem(unit, PARTS)
        return pltpu.make_async_remote_copy(
            src_ref=own.at[group * count + mat, part] if raw else from_left.at[group, unit],
            dst_ref=from_left.at[group, unit],
            send_sem=right_send.at[group, unit],
            recv_sem=right_recv.at[group, unit],
            device_id={"replica": rep + 1},
        )

    def left_copy(group, unit, raw=False):
        mat, part = unit // PARTS, lax.rem(unit, PARTS)
        return pltpu.make_async_remote_copy(
            src_ref=own.at[group * count + mat, part] if raw else from_right.at[group, unit],
            dst_ref=from_right.at[group, unit],
            send_sem=left_send.at[group, unit],
            recv_sem=left_recv.at[group, unit],
            device_id={"replica": rep - 1},
        )

    def gather_copy(unit, slot, target, place):
        mat, part = unit // PARTS, lax.rem(unit, PARTS)
        return pltpu.make_async_remote_copy(
            src_ref=outgoing.at[unit],
            dst_ref=gathered.at[mat // 2, part, slot],
            send_sem=gather_send.at[unit, place],
            recv_sem=gather_recv.at[mat // 2, slot, part],
            device_id={"fsdp": target},
        )

    def return_copy(mat):
        return pltpu.make_async_remote_copy(
            src_ref=finished.at[mat // 2],
            dst_ref=returned.at[mat],
            send_sem=return_send.at[mat // 2],
            recv_sem=return_recv.at[mat],
            device_id={"fsdp": partner},
        )

    def stored_copy(unit):
        mat, part = unit // PARTS, lax.rem(unit, PARTS)
        return pltpu.make_async_copy(
            stored.at[unit], stored_out.at[mat, :, columns(part)], stored_sem.at[unit]
        )

    def orth_copy(mat):
        return pltpu.make_async_copy(returned.at[mat], orth_out.at[mat], orth_sem.at[mat])

    def send_raw(unit):
        @pl.when(rep == 0)
        def _():
            for group in range(n_rep - 1, 0, -1):
                right_copy(group, unit, raw=True).start()

        @pl.when(rep == n_rep - 1)
        def _():
            for group in range(n_rep - 1):
                left_copy(group, unit, raw=True).start()

    def forward_right(unit):
        mat, part = unit // PARTS, lax.rem(unit, PARTS)
        for group in range(n_rep - 1, 1, -1):

            @pl.when(rep < group)
            def _():
                right_copy(group, unit).wait_recv()
                from_left[group, unit] = add_rows(
                    from_left[group, unit], own[group * count + mat, part]
                ).astype(jnp.bfloat16)
                right_copy(group, unit).start()

    def forward_left(unit):
        mat, part = unit // PARTS, lax.rem(unit, PARTS)
        for group in range(n_rep - 2):

            @pl.when(rep > group)
            def _():
                left_copy(group, unit).wait_recv()
                from_right[group, unit] = add_rows(
                    from_right[group, unit], own[group * count + mat, part]
                ).astype(jnp.bfloat16)
                left_copy(group, unit).start()

    def each_gather(unit, act):
        solver = lax.rem(unit // PARTS, 2)
        for step in range(1, chips):
            act(gather_copy(unit, me, lax.rem(chip + step, chips) * 2 + solver, step))

        @pl.when(core != solver)
        def _():
            act(gather_copy(unit, me, partner, 0))

    def finish_sum(unit):
        mat, part = unit // PARTS, lax.rem(unit, PARTS)
        total[...] = own[rep * count + mat, part].astype(jnp.float32)

        @pl.when(rep > 0)
        def _():
            right_copy(rep, unit).wait_recv()
            total[...] += from_left[rep, unit].astype(jnp.float32)

        @pl.when(rep < n_rep - 1)
        def _():
            left_copy(rep, unit).wait_recv()
            total[...] += from_right[rep, unit].astype(jnp.float32)

        summed = total[...]
        active = owners_ref[rep * count + mat] < n_fsdp
        decay = jnp.where(active, jnp.float32(MOMENTUM_DECAY), jnp.float32(1.0))
        gain = jnp.where(active, jnp.float32(1.0), jnp.float32(0.0))
        kept = (decay * old[mat, part].astype(jnp.float32) + gain * summed).astype(jnp.bfloat16)
        stored[unit] = kept
        stored_copy(unit).start()
        nesterov = (summed + MOMENTUM_DECAY * kept.astype(jnp.float32)).astype(jnp.bfloat16)
        outgoing[unit] = nesterov

        @pl.when(core == lax.rem(mat, 2))
        def _():
            gathered[mat // 2, part, me] = nesterov

        each_gather(unit, lambda copy: copy.start())

    def make_gram():
        rows = n_fsdp * row_count
        for low in range(0, rows, GRAM_TILE):
            high = min(low + GRAM_TILE, rows)
            block = lax.dot_general(
                iterate[low:, :],
                iterate[low:high, :],
                (((1,), (1,)), ((), ())),
                preferred_element_type=jnp.float32,
            )
            gram[low:, low:high] = block.astype(jnp.bfloat16)
            if high < rows:
                gram[low:high, high:] = block[high - low :, :].T.astype(jnp.bfloat16)

    def make_poly(rows):
        square = jnp.dot(gram[rows, :], gram[...], preferred_element_type=jnp.float32)
        poly[rows, :] = (
            COEFF_CUBIC * gram[rows, :].astype(jnp.float32) + COEFF_QUINTIC * square
        ).astype(jnp.bfloat16)

    def apply_poly(rows):
        product = jnp.dot(poly[rows, :], iterate[...], preferred_element_type=jnp.float32)
        return COEFF_LINEAR * iterate[rows, :].astype(jnp.float32) + product

    whole = pl.ds(0, n_fsdp * row_count)

    def normalize(mat):
        @pl.loop(1, n_fsdp)
        def _(step):
            for part in range(PARTS):
                gather_copy(mat * PARTS + part, lax.rem(me + step, n_fsdp), me, 0).wait_recv()

        scaled = gathered[mat // 2].astype(jnp.float32)
        frobenius = jnp.sqrt(jnp.sum(scaled * scaled))
        inverse = 1.0 / (frobenius + EPSILON)
        for part in range(PARTS):
            iterate[:, pl.ds(part * width, width)] = (
                (scaled[part] * inverse).reshape(n_fsdp * row_count, width).astype(jnp.bfloat16)
            )
        make_gram()

    def iterate_once():
        make_poly(whole)
        iterate[...] = apply_poly(whole).astype(jnp.bfloat16)

    def last_iterate(mat):
        make_gram()
        pair = pl.ds(pl.multiple_of(chip * (2 * row_count), 16), 2 * row_count)
        make_poly(pair)
        rows = apply_poly(pair).reshape(2, row_count, col_count).astype(jnp.bfloat16)
        for side in range(2):

            @pl.when(core == side)
            def _():
                returned[mat] = rows[side]
                finished[mat // 2] = rows[1 - side]

        return_copy(mat).start()

    ahead = min(LOOK_AHEAD, units)
    send_raw(0)
    for copy in loads[1:]:
        copy.wait()
    for unit in range(1, ahead):
        send_raw(unit)

    right_lag, left_lag = rep - 1, n_rep - 2 - rep
    sum_lag = jnp.maximum(right_lag, left_lag)

    @pl.loop(0, units + GATHER_TURNS + 2 + n_rep - 2)
    def _(turn):
        @pl.when(turn < units - ahead)
        def _():
            send_raw(turn + ahead)

        to_right, to_left, to_sum = turn - right_lag, turn - left_lag, turn - sum_lag

        @pl.when((rep > 0) & (to_right >= 0) & (to_right < units))
        def _():
            forward_right(to_right)

        @pl.when((rep < n_rep - 1) & (to_left >= 0) & (to_left < units))
        def _():
            forward_left(to_left)

        @pl.when((to_sum >= 0) & (to_sum < units))
        def _():
            finish_sum(to_sum)

        place = to_sum - GATHER_TURNS - (core + 1) * PARTS + 1
        mat = place // (2 * PARTS) * 2 + core
        stage = lax.rem(place, 2 * PARTS)
        ready = (place >= 0) & (mat < count)

        @pl.when(ready & (stage == 0))
        def _():
            normalize(mat)

        @pl.when(ready & (stage == 1))
        def _():
            iterate_once()

        @pl.when(ready & (stage == 2))
        def _():
            last_iterate(mat)

    @pl.loop(0, count)
    def _(mat):
        @pl.when(core != lax.rem(mat, 2))
        def _():
            return_copy(mat).wait_recv()

        orth_copy(mat).start()

    @pl.loop(0, units)
    def _(unit):
        for group in range(n_rep):

            @pl.when(rep < group)
            def _():
                right_copy(group, unit).wait_send()

            @pl.when(rep > group)
            def _():
                left_copy(group, unit).wait_send()

        each_gather(unit, lambda copy: copy.wait_send())
        stored_copy(unit).wait()

    @pl.loop(0, count)
    def _(mat):
        orth_copy(mat).wait()

    @pl.loop(0, count)
    def _(mat):
        @pl.when(core == lax.rem(mat, 2))
        def _():
            return_copy(mat).wait_send()


def fused_sum_and_orthogonalize(n_rep, n_fsdp, owners, grads, momentum):
    count, row_count, col_count = momentum.shape
    all_rows = n_fsdp * row_count
    units = count * PARTS
    jobs = (count + 1) // 2
    block = (row_count, col_count)
    piece = (row_count, col_count // PARTS)
    half = jnp.bfloat16
    shape = jax.ShapeDtypeStruct(momentum.shape, half)
    dma = pltpu.SemaphoreType.DMA
    return pl.pallas_call(
        functools.partial(fused_kernel, n_rep, n_fsdp, count),
        out_shape=(shape, shape),
        in_specs=[
            pl.BlockSpec(memory_space=pltpu.SMEM),
            pl.BlockSpec(memory_space=pl.ANY),
            pl.BlockSpec(memory_space=pl.ANY),
        ],
        out_specs=(pl.BlockSpec(memory_space=pl.ANY), pl.BlockSpec(memory_space=pl.ANY)),
        scratch_shapes=[
            pltpu.VMEM((n_rep * count, PARTS, *piece), half),
            pltpu.VMEM((count, PARTS, *piece), half),
            pltpu.VMEM((n_rep, units, *piece), half),
            pltpu.VMEM((n_rep, units, *piece), half),
            pltpu.VMEM(piece, jnp.float32),
            pltpu.VMEM((units, *piece), half),
            pltpu.VMEM((units, *piece), half),
            pltpu.VMEM((jobs, PARTS, n_fsdp, *piece), half),
            pltpu.VMEM((all_rows, col_count), half),
            pltpu.VMEM((all_rows, all_rows), half),
            pltpu.VMEM((all_rows, all_rows), half),
            pltpu.VMEM((jobs, *block), half),
            pltpu.VMEM((count, *block), half),
            dma((2, PARTS)),
            dma((n_rep, units)),
            dma((n_rep, units)),
            dma((n_rep, units)),
            dma((n_rep, units)),
            dma((units, n_fsdp // 2)),
            dma((jobs, n_fsdp, PARTS)),
            dma((jobs,)),
            dma((count,)),
            dma((units,)),
            dma((count,)),
        ],
        compiler_params=pltpu.CompilerParams(
            collective_id=0, has_side_effects=True, vmem_limit_bytes=KERNEL_VMEM
        ),
        name="sum_and_orthogonalize",
    )(owners, grads, momentum)


def finish_kernel(
    n_fsdp,
    update_scale,
    owners_ref,
    stored_ref,
    orth_ref,
    weight_ref,
    momentum_out,
    update_out,
    weight_out,
    stored,
    orth,
    weight,
    update,
    stepped,
    in_sem,
    out_sem,
):
    count = weight_ref.shape[0]
    offset = lax.axis_index("replica") * count
    loads, stores = [], []
    for mat in range(count):
        loads.append(
            [
                pltpu.make_async_copy(source.at[mat], held.at[mat], in_sem.at[place, mat])
                for place, (source, held) in enumerate(
                    ((orth_ref, orth), (weight_ref, weight), (stored_ref, stored))
                )
            ]
        )
        for copy in loads[-1]:
            copy.start()
    for mat in range(count):
        for copy in loads[mat]:
            copy.wait()
        on = jnp.where(owners_ref[offset + mat] < n_fsdp, jnp.float32(1.0), jnp.float32(0.0))
        held = orth[mat].astype(jnp.float32)
        update[mat] = ((update_scale * on) * held).astype(jnp.bfloat16)
        stepped[mat] = (
            weight[mat].astype(jnp.float32) * (1.0 - (LEARN_RATE * DECAY_RATE) * on)
            - (LEARN_RATE * update_scale * on) * held
        ).astype(jnp.bfloat16)
        for place, (held, target) in enumerate(
            ((stored, momentum_out), (update, update_out), (stepped, weight_out))
        ):
            copy = pltpu.make_async_copy(held.at[mat], target.at[mat], out_sem.at[place, mat])
            copy.start()
            stores.append(copy)
    for copy in stores:
        copy.wait()


def finish(n_fsdp, update_scale, owners, stored, orth, weight):
    count = weight.shape[0]
    anywhere = pl.BlockSpec(memory_space=pl.ANY)
    shape = jax.ShapeDtypeStruct(weight.shape, jnp.bfloat16)
    return pl.pallas_call(
        functools.partial(finish_kernel, n_fsdp, update_scale),
        out_shape=(shape, shape, shape),
        in_specs=[pl.BlockSpec(memory_space=pltpu.SMEM), anywhere, anywhere, anywhere],
        out_specs=(anywhere, anywhere, anywhere),
        scratch_shapes=[pltpu.VMEM(weight.shape, jnp.bfloat16)] * 5
        + [pltpu.SemaphoreType.DMA((3, count))] * 2,
        compiler_params=pltpu.CompilerParams(vmem_limit_bytes=KERNEL_VMEM),
        name="finish",
    )(owners, stored, orth, weight)


def by_collectives(grads, momentum, weight, active, update_scale):
    groups = lax.axis_size("fsdp")
    summed = lax.psum_scatter(
        grads[0], "replica", scatter_dimension=0, tiled=True
    ).astype(jnp.float32)
    local_count, row_count, col_count = momentum.shape
    keep_mask = active[:, None, None]
    old_momentum = momentum.astype(jnp.float32)
    new_momentum = jnp.where(
        keep_mask, MOMENTUM_DECAY * old_momentum + summed, old_momentum
    ).astype(jnp.bfloat16)
    stored = lax.optimization_barrier(new_momentum)
    outgoing = (summed + MOMENTUM_DECAY * stored.astype(jnp.float32)).astype(jnp.bfloat16)
    slots = -(-local_count // groups)
    padding = slots * groups - local_count
    packed = jnp.pad(outgoing, ((0, padding), (0, 0), (0, 0)))
    received = lax.all_to_all(packed, "fsdp", split_axis=0, concat_axis=1, tiled=True)
    orthogonal = newton_blocks(received)
    returned = lax.all_to_all(orthogonal, "fsdp", split_axis=1, concat_axis=0, tiled=True)
    restored = jnp.where(keep_mask, returned[:local_count].astype(jnp.float32), 0.0)
    update = (update_scale * restored).astype(jnp.bfloat16)
    old_weight = weight.astype(jnp.float32)
    stepped = old_weight * (1.0 - LEARN_RATE * DECAY_RATE) - LEARN_RATE * update_scale * restored
    new_weight = jnp.where(keep_mask, stepped, old_weight).astype(jnp.bfloat16)
    return (new_momentum, update, new_weight)


def on_device(grads, momentum, weight, owners):
    n_fsdp = lax.axis_size("fsdp")
    n_rep = lax.axis_size("replica")
    count, row_count, col_count = momentum.shape
    update_scale = UPDATE_RATIO * math.sqrt(max(row_count * n_fsdp, col_count))
    offset = lax.axis_index("replica") * count
    active = lax.dynamic_slice_in_dim(owners, offset, count) < n_fsdp
    held_bytes = 2 * row_count * col_count * (3 * n_rep * count + 5 * count + (count + 5) * n_fsdp // 2)
    fits = held_bytes < KERNEL_VMEM // 2 and row_count % ROW_TILE == 0
    fits = fits and col_count % (128 * PARTS) == 0
    if not fits or n_fsdp % 2 or n_rep < 2:
        return by_collectives(grads, momentum, weight, active, update_scale)
    stored, orth = fused_sum_and_orthogonalize(n_rep, n_fsdp, owners, grads[0], momentum)
    return finish(n_fsdp, update_scale, owners, stored, orth, weight)


def solution(mesh):
    in_specs = (
        P("replica", None, "fsdp", None),
        P("replica", "fsdp", None),
        P("replica", "fsdp", None),
        P(),
    )
    out_specs = (P("replica", "fsdp", None), P("replica", "fsdp", None), P("replica", "fsdp", None))
    return jax.shard_map(
        on_device, mesh=mesh, in_specs=in_specs, out_specs=out_specs, check_vma=False
    )
```
